128 devices in a mesh: section: 8 (over x, y_hi), seq: 4 (over y_lo, core), tensor: 4 (over z).
Axes of the slice: x: 4, y: 4 (y_hi: 2, y_lo: 2; y = y_hi * 2 + y_lo), z: 4, core: 2. Of those that a mesh axis runs over, the one named last changes fastest.
Arguments:
- patches: bfloat16 [32768, 1280], P(('section', 'seq'), 'tensor'), may hold values from -6 to 6
- norm_gain: float32 [1280], replicated, may hold values from 0.25 to 1.75
- w_in: bfloat16 [5120, 5120], P('seq', 'tensor'), may hold values from -0.078125 to 0.078125
- b_in: float32 [5120], P('tensor'), may hold values from -3 to 3
- w_out: bfloat16 [5120, 8192], P('tensor', 'seq'), may hold values from -0.078125 to 0.078125
- b_out: float32 [8192], P('tensor'), may hold values from -3 to 3
- text_rows: bfloat16 [32768, 8192], P(('section', 'seq'), 'tensor'), may hold values from -6 to 6
- dest_group: int32 [8192, 1], P(('section', 'seq')), may hold values from 0 to 31; in each aligned block of 256 rows (0 to 255, 256 to 511, ...) at most 16 rows name the same one
- dest_row: int32 [8192], P(('section', 'seq')), may hold values from 0 to 1023
- grad_rows: bfloat16 [32768, 8192], P(('section', 'seq'), 'tensor'), may hold values from -6 to 6
Outputs:
- llm_input: bfloat16 [32768, 8192], P(('section', 'seq'), 'tensor')
- grad_hidden: bfloat16 [8192, 5120], P(('section', 'seq'), 'tensor')
The draws below stay inside these ranges and needn't reach their ends.
Inputs may be any that keep to these rules, and one draw needn't show every extreme that they name: `dest_group`: among the rows of one device (aligned blocks of 256 rows) no index is named more than 16 times, a bound that some block reaches. `dest_row`: several vision tokens may land on one row; their embeddings are then all added.
All inputs are finite; a program needn't handle non-finite values.
Results may differ from the reference program's by a relative error of at most 0.008.
Values may be sent and summed in bfloat16 or wider, within the bound.
No kernel may reach another device: no remote copies, remote signals or barrier semaphores. Data moves between devices by JAX's collectives and lax.ppermute only.
A program may use at most 128 MiB of HBM per device.

```python
import math
import jax
import jax.numpy as jnp
import numpy as np
from jax import lax

D_VIS = 1280
D_LLM = 8192
V_DEV = 256
ROWS_DEV = 1024
MID = 5120
GROUPS = 32
CAP = 16
NV = 8192
NP = 32768
TOT_ROWS = 32768
N_TENSOR = 4


def plant(result, key, least, largest):
    spot = [jax.random.randint(jax.random.fold_in(key, axis), (), 0, length) for axis, length in enumerate(result.shape)]
    widest = result.shape.index(max(result.shape))
    beside = spot[:widest] + [(spot[widest] + 1) % result.shape[widest]] + spot[widest + 1:]
    return result.at[tuple(spot)].set(least).at[tuple(beside)].set(largest)


def steps_of(own_key, shape, cuts, low, largest):
    def one(dim, parts):
        steps = jax.random.uniform(jax.random.fold_in(jax.random.fold_in(own_key, 6), dim), (parts,), jnp.float32, low / len(cuts), largest / len(cuts))
        return jnp.repeat(jnp.exp(steps), shape[dim] // parts).reshape((-1,) + (1,) * (len(shape) - dim - 1))

    loudness = one(*cuts[0])
    for cut in cuts[1:]:
        loudness = loudness * one(*cut)
    return loudness


def assign_block(stream_key, own, number, rows, amount, top, limit, lean):
    ranking = jax.random.permutation(stream_key, amount)
    packed, ordinary = portions_of(amount, rows * top, limit, lean, True), portions_of(amount, rows * top, limit, lean, False)
    places = jnp.arange(amount)

    def named(tallies, offset_by):
        used = int((tallies > 0).sum())
        fixed = max(1, used // 4)
        moved = fixed + (places - fixed + offset_by * (used - fixed)) % max(1, amount - fixed)
        return jnp.zeros((amount,), jnp.int32).at[ranking[jnp.where(places < fixed, places, moved)]].set(jnp.asarray(tallies, jnp.int32))

    tallies = jnp.where(number % 4 == 0, named(packed, number // 4), named(ordinary, number - number // 4 - 1))
    mixed = jax.random.permutation(jax.random.fold_in(own, 3), amount)
    donor, taker = mixed[0:amount // 2 * 2:2], mixed[1:amount // 2 * 2:2]
    margin = jnp.minimum(tallies[donor] - 1, limit - tallies[taker]) // 2
    margin = jnp.where((donor == ranking[0]) | (taker == ranking[0]) | (tallies[taker] == 0), 0, jnp.maximum(margin, 0))
    moved = jax.random.randint(jax.random.fold_in(own, 4), (amount // 2,), 0, 1 << 20) % (margin + 1)
    tallies = tallies.at[donor].add(-moved).at[taker].add(moved)
    members = jnp.searchsorted(jnp.cumsum(tallies), jnp.arange(rows * top), side="right").astype(jnp.int32)
    grid = members.reshape(top, rows).T
    grid = grid[jax.random.permutation(jax.random.fold_in(own, 1), rows)]
    offset_by = jax.random.randint(jax.random.fold_in(own, 2), (rows, 1), 0, top)
    return jnp.take_along_axis(grid, (jnp.arange(top)[None, :] + offset_by) % top, axis=1)


def portions_of(amount, total, limit, lean, full):
    portions = [(1 << 20) // math.isqrt(grade ** lean) + 1 for grade in range(1, amount + 1)]
    largest = limit if full else min(limit, max(-(-total // amount), total * portions[0] // sum(portions)))
    least = 1 if total - largest >= amount - 1 else 0
    counts, spare = [largest] + [least] * (amount - 1), total - largest - least * (amount - 1)
    while spare > 0:
        movable = [i for i in range(1, amount) if counts[i] < largest] or [i for i in range(1, amount) if counts[i] < limit]
        mass, budget = sum([portions[i] for i in movable]), spare
        for i in movable:
            extra = min(limit - counts[i], max(1, budget * portions[i] // mass), spare)
            counts[i] = counts[i] + extra
            spare = spare - extra
    return np.array(counts)


def centred(key, extent, spread, most, pieces=(), dtype=jnp.bfloat16):
    array = jax.random.normal(key, extent, jnp.float32) * spread
    if len(pieces) > 0:
        array = steps_of(key, extent, pieces, -0.22, 0.18) * array
    return jnp.clip(array, min=-most, max=most).astype(dtype)


def setup_inputs(seed: int = 0) -> dict:
    keys = jax.random.split(jax.random.key(seed), 11)
    patches = centred(keys[0], (NP, D_VIS), 1.0, 6.0, ((0, 32), (1, 4)))
    norm_gain = jnp.clip(1.0 + 0.15 * jax.random.normal(keys[1], (D_VIS,), jnp.float32), 0.25, 1.75)
    w_in = centred(keys[2], (MID, MID), MID ** -0.5, 0.078125, ((0, 4), (1, 4)))
    b_in = centred(keys[3], (MID,), 0.5, 3.0, ((0, 4),), jnp.float32)
    w_out = centred(keys[4], (MID, D_LLM), MID ** -0.5, 0.078125, ((0, 4), (1, 4)))
    b_out = centred(keys[5], (D_LLM,), 0.5, 3.0, ((0, 4),), jnp.float32)
    text_rows = centred(keys[6], (TOT_ROWS, D_LLM), 1.0, 6.0, ((0, 32), (1, 4)))
    dest_group_keys = jax.random.split(jax.random.fold_in(keys[7], 1), NV // V_DEV)
    dest_group_turns = jax.random.permutation(jax.random.fold_in(keys[7], 3), NV // V_DEV)
    dest_group = jax.vmap(lambda own, number: assign_block(jax.random.fold_in(keys[7], 2), own, number, V_DEV, GROUPS, 1, CAP, 2))(dest_group_keys, dest_group_turns).reshape((NV, 1))
    dest_row = plant(jax.random.randint(keys[8], (NV,), 0, ROWS_DEV), jax.random.fold_in(keys[8], 1), 0, ROWS_DEV - 1).astype(jnp.int32)
    grad_rows = centred(keys[9], (TOT_ROWS, D_LLM), 1.0, 6.0, ((0, 32), (1, 4)))
    return {"patches": patches, "norm_gain": norm_gain, "w_in": w_in, "b_in": b_in, "w_out": w_out, "b_out": b_out, "text_rows": text_rows, "dest_group": dest_group, "dest_row": dest_row, "grad_rows": grad_rows}


def gelu_exact(x):
    return x * 0.5 * (1.0 + lax.erf(x * 0.7071067811865476))

def gelu_slope(x):
    return 0.5 * (1.0 + lax.erf(x * 0.7071067811865476)) + x * jnp.exp(-0.5 * x * x) * 0.3989422804014327

def reference(patches, norm_gain, w_in, b_in, w_out, b_out, text_rows, dest_group, dest_row, grad_rows):
    values = patches.astype(jnp.float32)
    scale = lax.rsqrt(lax.optimization_barrier(jnp.mean(values * values, axis=-1, keepdims=True)) + 1e-06)
    normed = (values * scale * norm_gain.astype(jnp.float32)).astype(jnp.bfloat16)
    merged = normed.reshape(NV, MID)
    pre = jnp.dot(merged, w_in, preferred_element_type=jnp.float32) + b_in.astype(jnp.float32)
    hidden = gelu_exact(pre).astype(jnp.bfloat16)
    width = MID // N_TENSOR
    total = jnp.zeros((NV, D_LLM), jnp.float32)
    for block in range(N_TENSOR):
        piece = jnp.dot(hidden[:, block * width:(block + 1) * width], w_out[block * width:(block + 1) * width], preferred_element_type=jnp.float32)
        rounded = lax.optimization_barrier(piece.astype(jnp.bfloat16))
        total = total + rounded.astype(jnp.float32)
    vision = (total + b_out.astype(jnp.float32)).astype(jnp.bfloat16)
    index = (dest_group[:, 0] * ROWS_DEV + dest_row).astype(jnp.int32)
    llm_input = text_rows.astype(jnp.float32).at[index].add(vision.astype(jnp.float32)).astype(jnp.bfloat16)
    grad_vision = grad_rows[index]
    back = jnp.dot(grad_vision, w_out.T, preferred_element_type=jnp.float32)
    grad_hidden = (back * gelu_slope(pre)).astype(jnp.bfloat16)
    return (llm_input, grad_hidden)
```

```python
import functools

import jax
import jax.numpy as jnp
from jax import lax
from jax.experimental import pallas as pl
from jax.experimental.pallas import tpu as pltpu
from jax.sharding import PartitionSpec as P

PLANE = ("section", "seq")
VMEM = pl.BlockSpec(memory_space=pltpu.VMEM)
SMEM = pl.BlockSpec(memory_space=pltpu.SMEM)
ANY = pl.BlockSpec(memory_space=pl.ANY)


def spot(x, y, c):
    return ((x % 4) * 4 + (y % 4)) * 2 + c


CHIPS = [(x, y, c) for x in range(4) for y in range(4) for c in range(2)]
CORE = [(spot(x, y, c), spot(x, y, 1 - c)) for x, y, c in CHIPS]
ALONG_Y = [(spot(x, y, c), spot(x, y + 1 - 2 * c, c)) for x, y, c in CHIPS]
ALONG_X = [(spot(x, y, c), spot(x + 1 - 2 * c, y, c)) for x, y, c in CHIPS]


def move(value, pairs):
    return lax.ppermute(value, PLANE, pairs)


def gather_pieces(own, axis, core, parity):
    size = own.shape[axis] // 2
    mine = lax.dynamic_slice_in_dim(own, core * size, size, axis)
    other = lax.dynamic_slice_in_dim(own, (1 - core) * size, size, axis)
    s1 = move(other, CORE)
    p1 = move(jnp.where(core == parity, mine, s1), ALONG_Y)
    p2 = move(p1, ALONG_X)
    s2 = move(mine, CORE)
    f1 = move(p1, CORE)
    f2 = move(p2, CORE)
    return own, s1, s2, p1, f1, p2, f2


def fetch(pieces, buffer, sems, axis):
    own, rest = pieces[0], pieces[1:]
    size = own.shape[axis] // 2
    halves = [own.at[pl.ds(h * size, size)] if axis == 0 else own.at[:, pl.ds(h * size, size)] for h in range(2)]
    copies = [pltpu.make_async_copy(s, buffer.at[i], sems.at[i]) for i, s in enumerate([*halves, *rest])]
    for copy in copies:
        copy.start()
    return copies


def merge_kernel(x_ref, gain_ref, out_ref):
    rows = 256
    tokens = rows // 4
    width = x_ref.shape[0]
    r = lax.broadcasted_iota(jnp.int32, (rows, rows), 1)
    q = lax.broadcasted_iota(jnp.int32, (rows, rows), 0)
    pick = (r == (q % tokens) * 4 + q // tokens).astype(jnp.bfloat16)
    for j in range(x_ref.shape[1] // rows):
        v = lax.dot_general(
            pick, x_ref[:, j * rows:(j + 1) * rows], (((1,), (1,)), ((), ())), preferred_element_type=jnp.float32
        )
        scale = lax.rsqrt(jnp.mean(v * v, axis=-1, keepdims=True) + 1e-06)
        n = (v * scale * gain_ref[...]).astype(jnp.bfloat16)
        for p in range(4):
            out_ref[j * tokens:(j + 1) * tokens, p * width:(p + 1) * width] = n[p * tokens:(p + 1) * tokens]


def merge(x, gain):
    width, rows = x.shape
    return pl.pallas_call(
        merge_kernel,
        out_shape=jax.ShapeDtypeStruct((rows // 4, 4 * width), jnp.bfloat16),
        in_specs=[VMEM, VMEM],
        out_specs=VMEM,
        compiler_params=pltpu.CompilerParams(vmem_limit_bytes=40 << 20),
        cost_estimate=pl.CostEstimate(flops=1 << 30, bytes_accessed=6 << 20, transcendentals=0),
    )(x, gain.reshape(1, -1))


def first_kernel(place_ref, x_ref, b_ref, *refs):
    pieces, (hidden_ref, slope_ref, buffer, acc, sems) = refs[:7], refs[7:]
    copies = fetch(pieces, buffer, sems, 0)
    depth = buffer.shape[1]
    for i, copy in enumerate(copies):
        copy.wait()
        at = pl.multiple_of(place_ref[i] * depth, 128)
        part = jnp.dot(x_ref[:, pl.ds(at, depth)], buffer[i], preferred_element_type=jnp.float32)
        if i == 0:
            acc[...] = part
        else:
            acc[...] += part
    pre = acc[...] + b_ref[...]
    phi = 0.5 * (1.0 + lax.erf(pre * 0.7071067811865476))
    hidden_ref[...] = (pre * phi).astype(jnp.bfloat16)
    slope_ref[...] = phi + pre * jnp.exp(-0.5 * pre * pre) * 0.3989422804014327


def first(place, x, b, pieces):
    rows, cols = x.shape[0], pieces[0].shape[1]
    return pl.pallas_call(
        first_kernel,
        out_shape=(
            jax.ShapeDtypeStruct((rows, cols), jnp.bfloat16),
            jax.ShapeDtypeStruct((rows, cols), jnp.float32),
        ),
        in_specs=[SMEM, VMEM, VMEM] + [ANY] * 7,
        out_specs=(VMEM, VMEM),
        scratch_shapes=[
            pltpu.VMEM((8,) + pieces[1].shape, jnp.bfloat16),
            pltpu.VMEM((rows, cols), jnp.float32),
            pltpu.SemaphoreType.DMA((8,)),
        ],
        compiler_params=pltpu.CompilerParams(vmem_limit_bytes=40 << 20),
        cost_estimate=pl.CostEstimate(flops=34 << 27, bytes_accessed=18 << 20, transcendentals=0),
    )(place, x, b.reshape(1, -1), *pieces)


def second_kernel(place_ref, h_ref, *refs):
    pieces, (out_ref, buffer, sems) = refs[:7], refs[7:]
    copies = fetch(pieces, buffer, sems, 1)
    width = buffer.shape[2]
    for i, copy in enumerate(copies):
        copy.wait()
        part = jnp.dot(h_ref[...], buffer[i], preferred_element_type=jnp.float32)
        at = pl.multiple_of((place_ref[i] % 2) * width, 128)
        out_ref[place_ref[i] // 2, :, pl.ds(at, width)] = part.astype(jnp.bfloat16)


def second(place, h, pieces):
    rows = h.shape[0]
    return pl.pallas_call(
        second_kernel,
        out_shape=jax.ShapeDtypeStruct((4, rows, pieces[0].shape[1]), jnp.bfloat16),
        in_specs=[SMEM, VMEM] + [ANY] * 7,
        out_specs=VMEM,
        scratch_shapes=[
            pltpu.VMEM((8,) + pieces[1].shape, jnp.bfloat16),
            pltpu.SemaphoreType.DMA((8,)),
        ],
        compiler_params=pltpu.CompilerParams(vmem_limit_bytes=40 << 20),
        cost_estimate=pl.CostEstimate(flops=54 << 27, bytes_accessed=26 << 20, transcendentals=0),
    )(place, h, *pieces)


def back_kernel(place_ref, g_ref, slope_ref, *refs):
    pieces, (out_ref, buffer, acc, sems) = refs[:7], refs[7:]
    copies = fetch(pieces, buffer, sems, 1)
    width = buffer.shape[2]
    for i, copy in enumerate(copies):
        copy.wait()
        at = pl.multiple_of((place_ref[i] % 2) * width, 128)
        part = lax.dot_general(
            g_ref[place_ref[i] // 2, :, pl.ds(at, width)],
            buffer[i],
            (((1,), (1,)), ((), ())),
            preferred_element_type=jnp.float32,
        )
        if i == 0:
            acc[...] = part
        else:
            acc[...] += part
    out_ref[...] = (acc[...] * slope_ref[...]).astype(jnp.bfloat16)


def back(place, g, slope, pieces):
    rows, cols = slope.shape
    return pl.pallas_call(
        back_kernel,
        out_shape=jax.ShapeDtypeStruct((rows, cols), jnp.bfloat16),
        in_specs=[SMEM, VMEM, VMEM] + [ANY] * 7,
        out_specs=VMEM,
        scratch_shapes=[
            pltpu.VMEM((8,) + pieces[1].shape, jnp.bfloat16),
            pltpu.VMEM((rows, cols), jnp.float32),
            pltpu.SemaphoreType.DMA((8,)),
        ],
        compiler_params=pltpu.CompilerParams(vmem_limit_bytes=40 << 20),
        cost_estimate=pl.CostEstimate(flops=54 << 27, bytes_accessed=28 << 20, transcendentals=0),
    )(place, g, slope, *pieces)


def body(patches, norm_gain, w_in, b_in, w_out, b_out, text_rows, dest_group, dest_row, grad_rows):
    seq = lax.axis_index("seq")
    core, y_lo = seq % 2, seq // 2
    parity = (lax.axis_index("section") // 2) % 2
    near, far = 2 * y_lo, 2 * (1 - y_lo)
    place = jnp.stack([
        2 * seq, 2 * seq + 1,
        2 * (near + 1 - core) + core, 2 * (near + 1 - core) + 1 - core,
        2 * (far + parity) + core, 2 * (far + parity) + 1 - core,
        2 * (far + 1 - parity) + core, 2 * (far + 1 - parity) + 1 - core,
    ]).astype(jnp.int32)

    whole = lax.all_gather(patches.T, "tensor", axis=0, tiled=True)
    in_pieces = gather_pieces(w_in, 0, core, parity)
    out_pieces = gather_pieces(w_out, 1, core, parity)

    merged = merge(whole, norm_gain)
    hidden, slope = first(place, merged, b_in, in_pieces)
    partial_terms = second(place, hidden, out_pieces)
    summed = lax.psum_scatter(partial_terms, "tensor", scatter_dimension=0, tiled=False).astype(jnp.float32)
    vision = (summed + b_out).astype(jnp.bfloat16)

    count = dest_row.shape[0]
    groups = lax.axis_size(PLANE)
    capacity = max(2, 2 * count // groups)
    width = vision.shape[1]
    target = dest_group.reshape(-1)
    member = (target[:, None] == jnp.arange(groups, dtype=jnp.int32)[None, :]).astype(jnp.int32)
    slot_of = jnp.sum((jnp.cumsum(member, axis=0) - 1) * member, axis=1)
    code = target * capacity + slot_of
    chosen = jnp.arange(groups * capacity, dtype=jnp.int32)[:, None] == code[None, :]
    select = chosen.astype(jnp.bfloat16)
    send_rows = jnp.sum(jnp.where(chosen, dest_row[None, :] + 1, 0), axis=1) - 1
    swap = functools.partial(lax.all_to_all, axis_name=PLANE, split_axis=0, concat_axis=0, tiled=True)
    got_rows = swap(send_rows.reshape(groups, capacity)).reshape(1, groups * capacity)
    nrows = text_rows.shape[0]
    place_rows = (jnp.arange(nrows, dtype=jnp.int32)[:, None] == got_rows).astype(jnp.bfloat16)
    picked = lax.dot_general(
        place_rows, grad_rows, (((0,), (0,)), ((), ())), preferred_element_type=jnp.float32
    ).astype(jnp.bfloat16)
    returned = swap(picked.reshape(groups, capacity, width)).reshape(groups * capacity, width)
    grad_vision = lax.dot_general(
        select, returned, (((0,), (0,)), ((), ())), preferred_element_type=jnp.float32
    ).astype(jnp.bfloat16)
    grad_full = lax.all_gather(grad_vision, "tensor", axis=0, tiled=False)

    send = jnp.dot(select, vision, preferred_element_type=jnp.float32).astype(jnp.bfloat16)
    got = swap(send.reshape(groups, capacity, width)).reshape(groups * capacity, width)
    placed = jnp.dot(place_rows, got, preferred_element_type=jnp.float32)
    llm_input = (text_rows.astype(jnp.float32) + placed).astype(jnp.bfloat16)
    grad_hidden = back(place, grad_full, slope, out_pieces)
    return (llm_input, grad_hidden)


def solution(mesh):
    in_specs = (
        P(("section", "seq"), "tensor"),
        P(),
        P("seq", "tensor"),
        P("tensor"),
        P("tensor", "seq"),
        P("tensor"),
        P(("section", "seq"), "tensor"),
        P(("section", "seq"), None),
        P(("section", "seq")),
        P(("section", "seq"), "tensor"),
    )
    out_specs = (P(("section", "seq"), "tensor"), P(("section", "seq"), "tensor"))
    return jax.shard_map(body, mesh=mesh, in_specs=in_specs, out_specs=out_specs, check_vma=False)
```

```python
import functools

import jax
import jax.numpy as jnp
from jax import lax
from jax.experimental import pallas as pl
from jax.experimental.pallas import tpu as pltpu
from jax.sharding import PartitionSpec as P

PLANE = ("section", "seq")
VMEM = pl.BlockSpec(memory_space=pltpu.VMEM)
SMEM = pl.BlockSpec(memory_space=pltpu.SMEM)
ANY = pl.BlockSpec(memory_space=pl.ANY)
BF16, F32 = jnp.bfloat16, jnp.float32
DIRECT = 384


TOKEN = jax.ShapeDtypeStruct((8, 128), F32)


def spot(x, y, c):
    return ((x % 4) * 4 + (y % 4)) * 2 + c


CHIPS = [(x, y, c) for x in range(4) for y in range(4) for c in range(2)]
CORE = [(spot(x, y, c), spot(x, y, 1 - c)) for x, y, c in CHIPS]
ALONG_Y = [(spot(x, y, c), spot(x, y + 1 - 2 * c, c)) for x, y, c in CHIPS]
ALONG_X = [(spot(x, y, c), spot(x + 1 - 2 * c, y, c)) for x, y, c in CHIPS]


def move(value, pairs):
    return lax.ppermute(value, PLANE, pairs)


def up(value):
    return lax.ppermute(value, "tensor", [(z, (z + 1) % 4) for z in range(4)])


def down(value):
    return lax.ppermute(value, "tensor", [(z, (z + 3) % 4) for z in range(4)])


def after(value, *others):
    return pl.pallas_call(
        lambda *refs: None,
        out_shape=jax.ShapeDtypeStruct(value.shape, value.dtype),
        in_specs=[ANY] * (1 + len(others)),
        out_specs=ANY,
        input_output_aliases={0: 0},
    )(value, *others)


def call(kernel, out_shape, in_specs, out_specs, scratch, flops, moved, *args, limit=46):
    return pl.pallas_call(
        kernel,
        out_shape=out_shape,
        in_specs=in_specs,
        out_specs=out_specs,
        scratch_shapes=scratch,
        compiler_params=pltpu.CompilerParams(vmem_limit_bytes=limit << 20),
        cost_estimate=pl.CostEstimate(flops=flops, bytes_accessed=moved, transcendentals=0),
    )(*args)


def parts_kernel(cuts, info_ref, own_ref, *refs):
    outs, sems = refs[-1 - len(cuts):-1], refs[-1]
    copies = []
    for i, (low, rows, left, cols) in enumerate(cuts):
        if low is None:
            low = pl.multiple_of(info_ref[3] * rows, rows)
        if left is None:
            left = pl.multiple_of(info_ref[3] * cols, cols)
        from_ref = own_ref.at[pl.ds(low, rows), pl.ds(left, cols)]
        copies.append(pltpu.make_async_copy(from_ref, outs[i], sems.at[i]))
    for copy in copies:
        copy.start()
    for copy in copies:
        copy.wait()


def parts_of(info, own, cuts, *tokens):
    out = [jax.ShapeDtypeStruct((rows, cols), BF16) for _, rows, _, cols in cuts]
    return call(
        functools.partial(parts_kernel, cuts), out, [SMEM] + [ANY] * (1 + len(tokens)), [VMEM] * len(out),
        [pltpu.SemaphoreType.DMA((len(out),))], 0, 2 * own.size, info, own, *tokens,
    )


def merge_kernel(info_ref, gain_ref, own_ref, *refs):
    parts, (out_ref, token_ref, x_ref, sems) = refs[:4], refs[4:]
    token_ref[...] = jnp.zeros_like(token_ref)
    z = info_ref[0]
    size = own_ref.shape[0] // 2
    width = 8 * size
    copies = []
    for i, (ref, step, half) in enumerate(zip((own_ref, *parts), (0, 3, 1, 2, 2), (0, 0, 0, 0, 1))):
        at = pl.multiple_of(((z + step) % 4) * 2 * size + half * size, 32)
        copies.append(pltpu.make_async_copy(ref, x_ref.at[pl.ds(at, ref.shape[0])], sems.at[i]))
    for copy in copies:
        copy.start()
    for copy in copies:
        copy.wait()
    rows = 256
    tokens = rows // 4
    r = lax.broadcasted_iota(jnp.int32, (rows, rows), 1)
    q = lax.broadcasted_iota(jnp.int32, (rows, rows), 0)
    pick = (r == (q % tokens) * 4 + q // tokens).astype(BF16)
    for j in range(x_ref.shape[1] // rows):
        v = lax.dot_general(
            pick, x_ref[:, j * rows:(j + 1) * rows], (((1,), (1,)), ((), ())), preferred_element_type=F32
        )
        scale = lax.rsqrt(jnp.mean(v * v, axis=-1, keepdims=True) + 1e-06)
        n = (v * scale * gain_ref[...]).astype(BF16)
        for p in range(4):
            out_ref[j * tokens:(j + 1) * tokens, p * width:(p + 1) * width] = n[p * tokens:(p + 1) * tokens]


def merge(info, gain, own, parts):
    width, rows = 4 * own.shape[0], own.shape[1]
    return call(
        merge_kernel,
        (jax.ShapeDtypeStruct((rows // 4, 4 * width), BF16), TOKEN),
        [SMEM, VMEM] + [ANY] * 5, (VMEM, VMEM),
        [pltpu.VMEM((width, rows), BF16), pltpu.SemaphoreType.DMA((5,))],
        1 << 30, 6 << 20,
        info, gain.reshape(1, -1), own, *parts,
    )


def load_parts(jobs, buffer, sems):
    copies = [pltpu.make_async_copy(ref, buffer.at[i], sems.at[i]) for i, (ref, _, _) in enumerate(jobs)]
    for copy in copies:
        copy.start()
    return copies


def add_parts(jobs, copies, x_ref, buffer, total):
    depth = buffer.shape[1]
    for i, (copy, (_, block, half)) in enumerate(zip(copies, jobs)):
        copy.wait()
        at = pl.multiple_of((2 * block + half) * depth, 128)
        part = jnp.dot(x_ref[:, pl.ds(at, depth)], buffer[i], preferred_element_type=F32)
        total = part if total is None else total + part
    return total


def first_near_kernel(info_ref, x_ref, own_ref, other_ref, out_ref, token_ref, buffer, sems):
    token_ref[...] = jnp.zeros_like(token_ref)
    y_lo, core = info_ref[1], info_ref[2]
    depth = buffer.shape[1]
    jobs = [
        (ref.at[pl.ds(half * depth, depth)], 2 * y_lo + low, half)
        for ref, low in ((own_ref, core), (other_ref, 1 - core)) for half in range(2)
    ]
    out_ref[...] = add_parts(jobs, load_parts(jobs, buffer, sems), x_ref, buffer, None)


def first_far_kernel(info_ref, x_ref, b_ref, near_ref, p1, f1, p2, f2, hidden_ref, slope_ref, buffer, sems):
    y_lo, core, parity = info_ref[1], info_ref[2], info_ref[3]
    far = 2 - 2 * y_lo
    jobs = [
        (p1, far + core, parity), (f1, far + 1 - core, parity),
        (p2, far + core, 1 - parity), (f2, far + 1 - core, 1 - parity),
    ]
    pre = add_parts(jobs, load_parts(jobs, buffer, sems), x_ref, buffer, near_ref[...] + b_ref[...])
    phi = 0.5 * (1.0 + lax.erf(pre * 0.7071067811865476))
    hidden_ref[...] = (pre * phi).astype(BF16)
    slope_ref[...] = phi + pre * jnp.exp(-0.5 * pre * pre) * 0.3989422804014327


def first_scratch(depth, cols):
    return [pltpu.VMEM((4, depth, cols), BF16), pltpu.SemaphoreType.DMA((4,))]


def first_near(info, x, near):
    rows, (depth, cols) = x.shape[0], near[0].shape
    return call(
        first_near_kernel,
        (jax.ShapeDtypeStruct((rows, cols), F32), TOKEN),
        [SMEM, VMEM, ANY, ANY], (VMEM, VMEM), first_scratch(depth // 2, cols), 17 << 27, 9 << 20,
        info, x, *near,
    )


def first_far(info, x, b, total, far):
    rows, (depth, cols) = x.shape[0], far[0].shape
    return call(
        first_far_kernel,
        (jax.ShapeDtypeStruct((rows, cols), BF16), jax.ShapeDtypeStruct((rows, cols), F32)),
        [SMEM, VMEM, VMEM, VMEM] + [ANY] * 4, (VMEM, VMEM), first_scratch(depth, cols), 17 << 27, 12 << 20,
        info, x, b.reshape(1, -1), total, *far,
    )


def near_kernel(info_ref, h_ref, own_ref, other_ref, out_ref, token_ref, buffer, sems):
    token_ref[...] = jnp.zeros_like(token_ref)
    core = info_ref[2]
    width = buffer.shape[2]
    jobs = [(ref, low, half) for ref, low in ((own_ref, core), (other_ref, 1 - core)) for half in range(2)]
    copies = [
        pltpu.make_async_copy(ref.at[:, pl.ds(half * width, width)], buffer.at[i], sems.at[i])
        for i, (ref, _, half) in enumerate(jobs)
    ]
    for copy in copies:
        copy.start()
    for i, (copy, (_, low, half)) in enumerate(zip(copies, jobs)):
        copy.wait()
        part = jnp.dot(h_ref[...], buffer[i], preferred_element_type=F32)
        out_ref[low, :, half * width:(half + 1) * width] = part.astype(BF16)


def far_kernel(info_ref, h_ref, near_ref, p1, f1, p2, f2, direct, crossed, *refs):
    outs, (buffer, whole, sems, out_sems) = refs[:8], refs[8:]
    z, y_lo, core, parity = info_ref[0], info_ref[1], info_ref[2], info_ref[3]
    width = buffer.shape[2]
    jobs = [
        (p1, core, parity), (f1, 1 - core, parity), (p2, core, 1 - parity), (f2, 1 - core, 1 - parity),
    ]
    for i, (ref, low, half) in enumerate(jobs):
        at = pl.ds(pl.multiple_of(half * width, width), width)
        straight = (direct, crossed)[i % 2].at[:, at]
        pltpu.make_async_copy(ref, buffer.at[i, pl.ds(DIRECT, ref.shape[0])], sems.at[i]).start()
        pltpu.make_async_copy(straight, buffer.at[i, pl.ds(0, DIRECT)], sems.at[i]).start()
    here = pltpu.make_async_copy(near_ref, whole.at[pl.ds(2 * y_lo, 2)], sems.at[4])
    here.start()
    for i, (_, low, half) in enumerate(jobs):
        pltpu.make_async_copy(buffer.at[i], buffer.at[i], sems.at[i]).wait()
        part = jnp.dot(h_ref[...], buffer[i], preferred_element_type=F32)
        at = pl.multiple_of(half * width, width)
        whole[2 - 2 * y_lo + low, :, pl.ds(at, width)] = part.astype(BF16)
    here.wait()
    copies = []
    for i, step in enumerate((2, 1, 3, 0)):
        for half in range(2):
            from_ref = whole.at[(z + step) % 4, :, pl.ds(half * width, width)]
            copies.append(pltpu.make_async_copy(from_ref, outs[2 * i + half], out_sems.at[2 * i + half]))
    for copy in copies:
        copy.start()
    for copy in copies:
        copy.wait()


def far_terms(info, h, near, pieces):
    rows, width = near.shape[1:]
    out = jax.ShapeDtypeStruct((rows, width // 2), BF16)
    return call(
        far_kernel,
        [out] * 8,
        [SMEM, VMEM, ANY] + [ANY] * 6, [ANY] * 8,
        [
            pltpu.VMEM((4, h.shape[1], width // 2), BF16),
            pltpu.VMEM((4, rows, width), BF16),
            pltpu.SemaphoreType.DMA((5,)),
            pltpu.SemaphoreType.DMA((8,)),
        ],
        27 << 27, 17 << 20,
        info, h, near, *pieces,
    )


def near_blocks(info, h, own, other):
    rows, width = own.shape
    return call(
        near_kernel,
        (jax.ShapeDtypeStruct((2, h.shape[0], width), BF16), TOKEN),
        [SMEM, VMEM, ANY, ANY], (VMEM, VMEM),
        [pltpu.VMEM((4, rows, width // 2), BF16), pltpu.SemaphoreType.DMA((4,))],
        27 << 27, 13 << 20,
        info, h, own, other,
    )


def send_kernel(code_ref, bias_ref, *refs):
    parts, (out_ref, sum_ref) = refs[:6], refs[6:]
    half = parts[0].shape[1]
    for i in range(2):
        at = slice(i * half, (i + 1) * half)
        total = sum(ref[...].astype(F32) for ref in parts[3 * i:3 * i + 3])
        sum_ref[:, at] = (total + bias_ref[:, at]).astype(BF16)
    slots, tokens = out_ref.shape[0], sum_ref.shape[0]
    chosen = lax.broadcasted_iota(jnp.int32, (slots, tokens), 0) == code_ref[...]
    out_ref[...] = jnp.dot(chosen.astype(BF16), sum_ref[...], preferred_element_type=F32).astype(BF16)


def rows_to_send(code, bias, parts, slots):
    rows, half = parts[0].shape
    return call(
        send_kernel,
        jax.ShapeDtypeStruct((slots, 2 * half), BF16),
        [VMEM] * 8, VMEM, [pltpu.VMEM((rows, 2 * half), BF16)],
        4 << 27, 6 << 20,
        code.reshape(1, -1), bias.reshape(1, -1), *parts,
    )


def pick_kernel(at_ref, rows_ref, out_ref, token_ref):
    token_ref[...] = jnp.zeros_like(token_ref)
    slots, rows = out_ref.shape[0], rows_ref.shape[0]
    named = (lax.broadcasted_iota(jnp.int32, (rows, slots), 0) == at_ref[...]).astype(BF16)
    out_ref[...] = lax.dot_general(
        named, rows_ref[...], (((0,), (0,)), ((), ())), preferred_element_type=F32
    ).astype(BF16)


def pick_rows(at, rows):
    slots, (count, width) = at.shape[1], rows.shape
    step = width // 4
    return pl.pallas_call(
        pick_kernel,
        grid=(4,),
        out_shape=(jax.ShapeDtypeStruct((slots, width), BF16), TOKEN),
        in_specs=[pl.BlockSpec((1, slots), lambda i: (0, 0)), pl.BlockSpec((count, step), lambda i: (0, i))],
        out_specs=(pl.BlockSpec((slots, step), lambda i: (0, i)), pl.BlockSpec((8, 128), lambda i: (0, 0))),
        compiler_params=pltpu.CompilerParams(vmem_limit_bytes=46 << 20),
        cost_estimate=pl.CostEstimate(flops=16 << 27, bytes_accessed=6 << 20, transcendentals=0),
    )(at, rows)


def place_kernel(at_ref, text_ref, got_ref, out_ref, token_ref):
    token_ref[...] = jnp.zeros_like(token_ref)
    rows, slots = out_ref.shape[0], got_ref.shape[0]
    named = (lax.broadcasted_iota(jnp.int32, (rows, slots), 0) == at_ref[...]).astype(BF16)
    added = jnp.dot(named, got_ref[...], preferred_element_type=F32)
    out_ref[...] = (text_ref[...].astype(F32) + added).astype(BF16)


def place_rows(at, text, got):
    (count, width), slots = text.shape, got.shape[0]
    step = width // 4
    return pl.pallas_call(
        place_kernel,
        grid=(4,),
        out_shape=(jax.ShapeDtypeStruct(text.shape, BF16), TOKEN),
        in_specs=[
            pl.BlockSpec((1, slots), lambda i: (0, 0)),
            pl.BlockSpec((count, step), lambda i: (0, i)),
            pl.BlockSpec((slots, step), lambda i: (0, i)),
        ],
        out_specs=(pl.BlockSpec((count, step), lambda i: (0, i)), pl.BlockSpec((8, 128), lambda i: (0, 0))),
        compiler_params=pltpu.CompilerParams(vmem_limit_bytes=60 << 20),
        cost_estimate=pl.CostEstimate(flops=16 << 27, bytes_accessed=10 << 20, transcendentals=0),
    )(at, text, got)


def home_kernel(code_ref, rows_ref, _, *outs):
    slots, tokens = rows_ref.shape[0], outs[0].shape[0]
    chosen = lax.broadcasted_iota(jnp.int32, (slots, tokens), 0) == code_ref[...]
    width = outs[0].shape[1]
    for i, out_ref in enumerate(outs):
        out_ref[...] = lax.dot_general(
            chosen.astype(BF16),
            rows_ref[:, i * width:(i + 1) * width],
            (((0,), (0,)), ((), ())),
            preferred_element_type=F32,
        ).astype(BF16)


def gradients_home(code, rows, token):
    half = jax.ShapeDtypeStruct((code.shape[0], rows.shape[1] // 2), BF16)
    return call(
        home_kernel, (half, half), [VMEM, VMEM, ANY], (VMEM, VMEM), [],
        4 << 27, 3 << 20, code.reshape(1, -1), rows, token,
    )


def load_any(slot, sem, info_ref, block, half, own, other, p1, f1, p2, f2, direct, crossed):
    y_lo, core, parity = info_ref[1], info_ref[2], info_ref[3]
    width = slot.shape[1]
    at = pl.ds(half * width, width)
    near, low = block // 2 == y_lo, block % 2
    for ref, same in ((own, low == core), (other, low != core)):
        @pl.when(jnp.logical_and(near, same))
        def _():
            pltpu.make_async_copy(ref.at[:, at], slot, sem).start()

    far = jnp.logical_not(near)
    for ref, same in ((direct, low == core), (crossed, low != core)):
        @pl.when(jnp.logical_and(far, same))
        def _():
            pltpu.make_async_copy(ref.at[:, at], slot.at[pl.ds(0, DIRECT)], sem).start()

    for ref, test in (
        (p1, jnp.logical_and(low == core, half == parity)),
        (f1, jnp.logical_and(low != core, half == parity)),
        (p2, jnp.logical_and(low == core, half != parity)),
        (f2, jnp.logical_and(low != core, half != parity)),
    ):
        @pl.when(jnp.logical_and(far, test))
        def _():
            pltpu.make_async_copy(ref, slot.at[pl.ds(DIRECT, ref.shape[0])], sem).start()


def back_kernel(steps, starts, ends, info_ref, *refs):
    refs = list(refs)
    grads = [refs.pop(0) for _ in steps]
    before = None if starts else refs.pop(0)
    slope_ref = refs.pop(0) if ends else None
    pieces = [refs.pop(0) for _ in range(8)]
    out_ref, buffer, sems = refs[-3:]
    z = info_ref[0]
    for i, (step, half) in enumerate(steps):
        load_any(buffer.at[i], sems.at[i], info_ref, (z + step) % 4, half, *pieces)
    total = None if starts else before[...]
    for i in range(len(steps)):
        pltpu.make_async_copy(buffer.at[i], buffer.at[i], sems.at[i]).wait()
        part = lax.dot_general(grads[i][...], buffer[i], (((1,), (1,)), ((), ())), preferred_element_type=F32)
        total = part if total is None else total + part
    out_ref[...] = (total * slope_ref[...]).astype(BF16) if ends else total


def back(info, steps, grads, before, slope, pieces, *tokens):
    rows, (depth, width) = grads[0].shape[0], pieces[0].shape
    extra = [a for a in (before, slope) if a is not None]
    out = jax.ShapeDtypeStruct((rows, depth), F32 if slope is None else BF16)
    return call(
        functools.partial(back_kernel, steps, before is None, slope is not None),
        out,
        [SMEM] + [VMEM] * (len(grads) + len(extra)) + [ANY] * (8 + len(tokens)), VMEM,
        [pltpu.VMEM((len(steps), depth, width // 2), BF16), pltpu.SemaphoreType.DMA((len(steps),))],
        len(steps) * 7 << 27, len(steps) * 3 << 20,
        info, *grads, *extra, *pieces, *tokens, limit=60 if slope is not None else 46,
    )


def body(patches, norm_gain, w_in, b_in, w_out, b_out, text_rows, dest_group, dest_row, grad_rows):
    seq = lax.axis_index("seq")
    core, y_lo = seq % 2, seq // 2
    parity = (lax.axis_index("section") // 2) % 2
    z = lax.axis_index("tensor")
    info = jnp.stack([z, y_lo, core, parity]).astype(jnp.int32)

    count = dest_row.shape[0]
    groups = lax.axis_size(PLANE)
    capacity = max(2, 2 * count // groups)
    width = grad_rows.shape[1]
    target = dest_group.reshape(-1)
    member = (target[:, None] == jnp.arange(groups, dtype=jnp.int32)[None, :]).astype(jnp.int32)
    slot_of = jnp.sum((jnp.cumsum(member, axis=0) - 1) * member, axis=1)
    code = target * capacity + slot_of
    chosen = jnp.arange(groups * capacity, dtype=jnp.int32)[:, None] == code[None, :]
    send_rows = jnp.sum(jnp.where(chosen, dest_row[None, :] + 1, 0), axis=1) - 1
    swap = functools.partial(lax.all_to_all, axis_name=PLANE, split_axis=0, concat_axis=0, tiled=True)
    got_rows = swap(send_rows.reshape(groups, capacity)).reshape(1, groups * capacity)

    rows, cols = w_in.shape
    p1_in = move(parts_of(info, w_in, [(None, rows // 2, 0, cols)])[0], ALONG_Y)
    other_in = move(w_in, CORE)
    other_out = move(w_out, CORE)
    x = patches.T
    size = x.shape[0] // 2
    xa, xb = up(x), down(x)
    xc1, xc2 = up(xa[:size]), down(xb[size:])
    rows, cols = w_out.shape
    relayed, straight = parts_of(
        info, w_out, [(DIRECT, rows - DIRECT, None, cols // 2), (0, DIRECT, 0, cols)]
    )
    p1_in = after(p1_in, relayed, other_in, other_out, got_rows, xa, xb)
    p2_in = move(p1_in, ALONG_X)
    f1_in = move(p1_in, CORE)
    p1 = move(after(relayed, p1_in), ALONG_Y)
    picked, picked_token = pick_rows(got_rows, grad_rows)
    merged, merged_token = merge(info, norm_gain, x, (xa, xb, xc1, xc2))
    total, first_token = first_near(info, merged, (w_in, other_in))
    p1 = after(p1, first_token, picked_token)
    p2 = move(p1, ALONG_X)
    f1 = move(p1, CORE)
    direct = move(after(straight, p1), ALONG_Y)

    hidden, slope = first_far(info, merged, b_in, total, (p1_in, f1_in, p2_in, move(p2_in, CORE)))
    near, near_token = near_blocks(info, hidden, w_out, other_out)
    p2, direct = after(p2, near_token), after(direct, near_token)
    picked = after(picked, p2, direct)
    f2 = move(p2, CORE)
    crossed = move(direct, CORE)
    t20, t21, t10, t11, t30, t31, t00, t01 = far_terms(info, hidden, near, (p1, f1, p2, f2, direct, crossed))

    returned = swap(picked.reshape(groups, capacity, width)).reshape(groups * capacity, width)

    def add(one, two):
        return (one.astype(F32) + two.astype(F32)).astype(BF16)

    sa1, sa2 = up(t20), down(t21)
    sb1, sb2 = up(t11), down(t30)
    sc1, sc2 = up(add(t10, sa1)), down(add(t31, sa2))
    send = rows_to_send(code, b_out, (t00, sb2, sc1, t01, sb1, sc2), groups * capacity)
    got = swap(send.reshape(groups, capacity, width)).reshape(groups * capacity, width)

    g1, g2 = gradients_home(code, returned, send)
    ga1, ga2 = up(g1), down(g2)
    gb1, gb2 = up(g2), down(g1)
    gc1, gc2 = up(ga1), down(ga2)
    pieces = (w_out, other_out, p1, f1, p2, f2, direct, crossed)
    total = back(info, ((0, 0), (0, 1)), (g1, g2), None, None, pieces)
    total = back(info, ((3, 0), (3, 1), (1, 0), (1, 1)), (ga1, gb1, gb2, ga2), total, None, pieces)
    llm_input, placed = place_rows(got_rows, text_rows, got)
    grad_hidden = back(info, ((2, 0), (2, 1)), (gc1, gc2), total, slope, pieces, placed)

    return (llm_input, grad_hidden)


def solution(mesh):
    in_specs = (
        P(("section", "seq"), "tensor"),
        P(),
        P("seq", "tensor"),
        P("tensor"),
        P("tensor", "seq"),
        P("tensor"),
        P(("section", "seq"), "tensor"),
        P(("section", "seq"), None),
        P(("section", "seq")),
        P(("section", "seq"), "tensor"),
    )
    out_specs = (P(("section", "seq"), "tensor"), P(("section", "seq"), "tensor"))
    return jax.shard_map(body, mesh=mesh, in_specs=in_specs, out_specs=out_specs, check_vma=False)
```

```python
import functools

import jax
import jax.numpy as jnp
from jax import lax
from jax.experimental import pallas as pl
from jax.experimental.pallas import tpu as pltpu
from jax.sharding import PartitionSpec as P

PLANE = ("section", "seq")
VMEM = pl.BlockSpec(memory_space=pltpu.VMEM)
SMEM = pl.BlockSpec(memory_space=pltpu.SMEM)
ANY = pl.BlockSpec(memory_space=pl.ANY)
BF16, F32 = jnp.bfloat16, jnp.float32
DIRECT = 384


TOKEN = jax.ShapeDtypeStruct((8, 128), F32)


def spot(x, y, c):
    return ((x % 4) * 4 + (y % 4)) * 2 + c


CHIPS = [(x, y, c) for x in range(4) for y in range(4) for c in range(2)]
CORE = [(spot(x, y, c), spot(x, y, 1 - c)) for x, y, c in CHIPS]
ALONG_Y = [(spot(x, y, c), spot(x, y + 1 - 2 * c, c)) for x, y, c in CHIPS]
ALONG_X = [(spot(x, y, c), spot(x + 1 - 2 * c, y, c)) for x, y, c in CHIPS]


def move(value, pairs):
    return lax.ppermute(value, PLANE, pairs)


def up(value):
    return lax.ppermute(value, "tensor", [(z, (z + 1) % 4) for z in range(4)])


def down(value):
    return lax.ppermute(value, "tensor", [(z, (z + 3) % 4) for z in range(4)])


def after(value, *others):
    return pl.pallas_call(
        lambda *refs: None,
        out_shape=jax.ShapeDtypeStruct(value.shape, value.dtype),
        in_specs=[ANY] * (1 + len(others)),
        out_specs=ANY,
        input_output_aliases={0: 0},
    )(value, *others)


def call(kernel, out_shape, in_specs, out_specs, scratch, flops, moved, *args, limit=46):
    return pl.pallas_call(
        kernel,
        out_shape=out_shape,
        in_specs=in_specs,
        out_specs=out_specs,
        scratch_shapes=scratch,
        compiler_params=pltpu.CompilerParams(vmem_limit_bytes=limit << 20),
        cost_estimate=pl.CostEstimate(flops=flops, bytes_accessed=moved, transcendentals=0),
    )(*args)


def parts_kernel(cuts, info_ref, own_ref, *refs):
    outs, sems = refs[-1 - len(cuts):-1], refs[-1]
    copies = []
    for i, (low, rows, left, cols) in enumerate(cuts):
        if low is None:
            low = pl.multiple_of(info_ref[3] * rows, rows)
        if left is None:
            left = pl.multiple_of(info_ref[3] * cols, cols)
        from_ref = own_ref.at[pl.ds(low, rows), pl.ds(left, cols)]
        copies.append(pltpu.make_async_copy(from_ref, outs[i], sems.at[i]))
    for copy in copies:
        copy.start()
    for copy in copies:
        copy.wait()


def parts_of(info, own, cuts, *tokens):
    out = [jax.ShapeDtypeStruct((rows, cols), BF16) for _, rows, _, cols in cuts]
    return call(
        functools.partial(parts_kernel, cuts), out, [SMEM] + [ANY] * (1 + len(tokens)), [VMEM] * len(out),
        [pltpu.SemaphoreType.DMA((len(out),))], 0, 2 * own.size, info, own, *tokens,
    )


def merge_kernel(info_ref, gain_ref, own_ref, *refs):
    parts, (out_ref, token_ref, x_ref, sems) = refs[:4], refs[4:]
    token_ref[...] = jnp.zeros_like(token_ref)
    z = info_ref[0]
    size = own_ref.shape[0] // 2
    width = 8 * size
    copies = []
    for i, (ref, step, half) in enumerate(zip((own_ref, *parts), (0, 3, 1, 2, 2), (0, 0, 0, 0, 1))):
        at = pl.multiple_of(((z + step) % 4) * 2 * size + half * size, 32)
        copies.append(pltpu.make_async_copy(ref, x_ref.at[pl.ds(at, ref.shape[0])], sems.at[i]))
    for copy in copies:
        copy.start()
    for copy in copies:
        copy.wait()
    rows = 256
    tokens = rows // 4
    r = lax.broadcasted_iota(jnp.int32, (rows, rows), 1)
    q = lax.broadcasted_iota(jnp.int32, (rows, rows), 0)
    pick = (r == (q % tokens) * 4 + q // tokens).astype(BF16)
    for j in range(x_ref.shape[1] // rows):
        v = lax.dot_general(
            pick, x_ref[:, j * rows:(j + 1) * rows], (((1,), (1,)), ((), ())), preferred_element_type=F32
        )
        scale = lax.rsqrt(jnp.mean(v * v, axis=-1, keepdims=True) + 1e-06)
        n = (v * scale * gain_ref[...]).astype(BF16)
        for p in range(4):
            out_ref[j * tokens:(j + 1) * tokens, p * width:(p + 1) * width] = n[p * tokens:(p + 1) * tokens]


def merge(info, gain, own, parts):
    width, rows = 4 * own.shape[0], own.shape[1]
    return call(
        merge_kernel,
        (jax.ShapeDtypeStruct((rows // 4, 4 * width), BF16), TOKEN),
        [SMEM, VMEM] + [ANY] * 5, (VMEM, VMEM),
        [pltpu.VMEM((width, rows), BF16), pltpu.SemaphoreType.DMA((5,))],
        1 << 30, 6 << 20,
        info, gain.reshape(1, -1), own, *parts,
    )


def load_parts(jobs, buffer, sems):
    copies = [pltpu.make_async_copy(ref, buffer.at[i], sems.at[i]) for i, (ref, _, _) in enumerate(jobs)]
    for copy in copies:
        copy.start()
    return copies


def add_parts(jobs, copies, x_ref, buffer, total):
    depth = buffer.shape[1]
    for i, (copy, (_, block, half)) in enumerate(zip(copies, jobs)):
        copy.wait()
        at = pl.multiple_of((2 * block + half) * depth, 128)
        part = jnp.dot(x_ref[:, pl.ds(at, depth)], buffer[i], preferred_element_type=F32)
        total = part if total is None else total + part
    return total


def first_near_kernel(info_ref, x_ref, own_ref, other_ref, out_ref, token_ref, buffer, sems):
    token_ref[...] = jnp.zeros_like(token_ref)
    y_lo, core = info_ref[1], info_ref[2]
    depth = buffer.shape[1]
    jobs = [
        (ref.at[pl.ds(half * depth, depth)], 2 * y_lo + low, half)
        for ref, low in ((own_ref, core), (other_ref, 1 - core)) for half in range(2)
    ]
    out_ref[...] = add_parts(jobs, load_parts(jobs, buffer, sems), x_ref, buffer, None)


def first_far_kernel(info_ref, x_ref, b_ref, near_ref, p1, f1, p2, f2, hidden_ref, slope_ref, buffer, sems):
    y_lo, core, parity = info_ref[1], info_ref[2], info_ref[3]
    far = 2 - 2 * y_lo
    jobs = [
        (p1, far + core, parity), (f1, far + 1 - core, parity),
        (p2, far + core, 1 - parity), (f2, far + 1 - core, 1 - parity),
    ]
    pre = add_parts(jobs, load_parts(jobs, buffer, sems), x_ref, buffer, near_ref[...] + b_ref[...])
    phi = 0.5 * (1.0 + lax.erf(pre * 0.7071067811865476))
    hidden_ref[...] = (pre * phi).astype(BF16)
    slope_ref[...] = phi + pre * jnp.exp(-0.5 * pre * pre) * 0.3989422804014327


def first_scratch(depth, cols):
    return [pltpu.VMEM((4, depth, cols), BF16), pltpu.SemaphoreType.DMA((4,))]


def first_near(info, x, near):
    rows, (depth, cols) = x.shape[0], near[0].shape
    return call(
        first_near_kernel,
        (jax.ShapeDtypeStruct((rows, cols), F32), TOKEN),
        [SMEM, VMEM, ANY, ANY], (VMEM, VMEM), first_scratch(depth // 2, cols), 17 << 27, 9 << 20,
        info, x, *near,
    )


def first_far(info, x, b, total, far):
    rows, (depth, cols) = x.shape[0], far[0].shape
    return call(
        first_far_kernel,
        (jax.ShapeDtypeStruct((rows, cols), BF16), jax.ShapeDtypeStruct((rows, cols), F32)),
        [SMEM, VMEM, VMEM, VMEM] + [ANY] * 4, (VMEM, VMEM), first_scratch(depth, cols), 17 << 27, 12 << 20,
        info, x, b.reshape(1, -1), total, *far,
    )


def near_kernel(info_ref, h_ref, own_ref, other_ref, out_ref, token_ref, buffer, sems):
    token_ref[...] = jnp.zeros_like(token_ref)
    core = info_ref[2]
    width = buffer.shape[2]
    jobs = [(ref, low, half) for ref, low in ((own_ref, core), (other_ref, 1 - core)) for half in range(2)]
    copies = [
        pltpu.make_async_copy(ref.at[:, pl.ds(half * width, width)], buffer.at[i], sems.at[i])
        for i, (ref, _, half) in enumerate(jobs)
    ]
    for copy in copies:
        copy.start()
    for i, (copy, (_, low, half)) in enumerate(zip(copies, jobs)):
        copy.wait()
        part = jnp.dot(h_ref[...], buffer[i], preferred_element_type=F32)
        out_ref[low, :, half * width:(half + 1) * width] = part.astype(BF16)


def far_kernel(info_ref, h_ref, near_ref, p1, f1, p2, f2, direct, crossed, *refs):
    outs, (buffer, whole, sems, out_sems) = refs[:8], refs[8:]
    z, y_lo, core, parity = info_ref[0], info_ref[1], info_ref[2], info_ref[3]
    width = buffer.shape[2]
    jobs = [
        (p1, core, parity), (f1, 1 - core, parity), (p2, core, 1 - parity), (f2, 1 - core, 1 - parity),
    ]
    for i, (ref, low, half) in enumerate(jobs):
        at = pl.ds(pl.multiple_of(half * width, width), width)
        straight = (direct, crossed)[i % 2].at[:, at]
        pltpu.make_async_copy(ref, buffer.at[i, pl.ds(DIRECT, ref.shape[0])], sems.at[i]).start()
        pltpu.make_async_copy(straight, buffer.at[i, pl.ds(0, DIRECT)], sems.at[i]).start()
    here = pltpu.make_async_copy(near_ref, whole.at[pl.ds(2 * y_lo, 2)], sems.at[4])
    here.start()
    for i, (_, low, half) in enumerate(jobs):
        pltpu.make_async_copy(buffer.at[i], buffer.at[i], sems.at[i]).wait()
        part = jnp.dot(h_ref[...], buffer[i], preferred_element_type=F32)
        at = pl.multiple_of(half * width, width)
        whole[2 - 2 * y_lo + low, :, pl.ds(at, width)] = part.astype(BF16)
    here.wait()
    copies = []
    for i, step in enumerate((2, 1, 3, 0)):
        for half in range(2):
            from_ref = whole.at[(z + step) % 4, :, pl.ds(half * width, width)]
            copies.append(pltpu.make_async_copy(from_ref, outs[2 * i + half], out_sems.at[2 * i + half]))
    for copy in copies:
        copy.start()
    for copy in copies:
        copy.wait()


def far_terms(info, h, near, pieces):
    rows, width = near.shape[1:]
    out = jax.ShapeDtypeStruct((rows, width // 2), BF16)
    return call(
        far_kernel,
        [out] * 8,
        [SMEM, VMEM, ANY] + [ANY] * 6, [ANY] * 8,
        [
            pltpu.VMEM((4, h.shape[1], width // 2), BF16),
            pltpu.VMEM((4, rows, width), BF16),
            pltpu.SemaphoreType.DMA((5,)),
            pltpu.SemaphoreType.DMA((8,)),
        ],
        27 << 27, 17 << 20,
        info, h, near, *pieces,
    )


def near_blocks(info, h, own, other):
    rows, width = own.shape
    return call(
        near_kernel,
        (jax.ShapeDtypeStruct((2, h.shape[0], width), BF16), TOKEN),
        [SMEM, VMEM, ANY, ANY], (VMEM, VMEM),
        [pltpu.VMEM((4, rows, width // 2), BF16), pltpu.SemaphoreType.DMA((4,))],
        27 << 27, 13 << 20,
        info, h, own, other,
    )


def send_kernel(code_ref, bias_ref, _, *refs):
    parts, (out_ref, sum_ref) = refs[:6], refs[6:]
    half = parts[0].shape[1]
    for i in range(2):
        at = slice(i * half, (i + 1) * half)
        total = sum(ref[...].astype(F32) for ref in parts[3 * i:3 * i + 3])
        sum_ref[:, at] = (total + bias_ref[:, at]).astype(BF16)
    slots, tokens = out_ref.shape[0], sum_ref.shape[0]
    chosen = lax.broadcasted_iota(jnp.int32, (slots, tokens), 0) == code_ref[...]
    out_ref[...] = jnp.dot(chosen.astype(BF16), sum_ref[...], preferred_element_type=F32).astype(BF16)


def rows_to_send(code, bias, token, parts, slots):
    rows, half = parts[0].shape
    return call(
        send_kernel,
        jax.ShapeDtypeStruct((slots, 2 * half), BF16),
        [VMEM, VMEM, ANY] + [VMEM] * 6, VMEM, [pltpu.VMEM((rows, 2 * half), BF16)],
        4 << 27, 6 << 20,
        code.reshape(1, -1), bias.reshape(1, -1), token, *parts,
    )


def pick_kernel(at_ref, rows_ref, out_ref, token_ref):
    token_ref[...] = jnp.zeros_like(token_ref)
    slots, rows = out_ref.shape[0], rows_ref.shape[0]
    named = (lax.broadcasted_iota(jnp.int32, (rows, slots), 0) == at_ref[...]).astype(BF16)
    out_ref[...] = lax.dot_general(
        named, rows_ref[...], (((0,), (0,)), ((), ())), preferred_element_type=F32
    ).astype(BF16)


def pick_rows(at, rows):
    slots, (count, width) = at.shape[1], rows.shape
    step = width // 4
    return pl.pallas_call(
        pick_kernel,
        grid=(4,),
        out_shape=(jax.ShapeDtypeStruct((slots, width), BF16), TOKEN),
        in_specs=[pl.BlockSpec((1, slots), lambda i: (0, 0)), pl.BlockSpec((count, step), lambda i: (0, i))],
        out_specs=(pl.BlockSpec((slots, step), lambda i: (0, i)), pl.BlockSpec((8, 128), lambda i: (0, 0))),
        compiler_params=pltpu.CompilerParams(vmem_limit_bytes=46 << 20),
        cost_estimate=pl.CostEstimate(flops=16 << 27, bytes_accessed=6 << 20, transcendentals=0),
    )(at, rows)


def place_kernel(at_ref, text_ref, got_ref, out_ref, token_ref):
    token_ref[...] = jnp.zeros_like(token_ref)
    rows, slots = out_ref.shape[0], got_ref.shape[0]
    row = lax.broadcasted_iota(jnp.int32, (rows, slots), 0) + pl.program_id(0) * rows
    added = jnp.dot((row == at_ref[...]).astype(BF16), got_ref[...], preferred_element_type=F32)
    out_ref[...] = (text_ref[...].astype(F32) + added).astype(BF16)


def place_rows(at, text, got):
    (count, width), slots = text.shape, got.shape[0]
    step = count // 4
    return pl.pallas_call(
        place_kernel,
        grid=(4,),
        out_shape=(jax.ShapeDtypeStruct(text.shape, BF16), TOKEN),
        in_specs=[
            pl.BlockSpec((1, slots), lambda i: (0, 0)),
            pl.BlockSpec((step, width), lambda i: (i, 0)),
            pl.BlockSpec((slots, width), lambda i: (0, 0)),
        ],
        out_specs=(pl.BlockSpec((step, width), lambda i: (i, 0)), pl.BlockSpec((8, 128), lambda i: (0, 0))),
        compiler_params=pltpu.CompilerParams(vmem_limit_bytes=56 << 20),
        cost_estimate=pl.CostEstimate(flops=16 << 27, bytes_accessed=10 << 20, transcendentals=0),
    )(at, text, got)


def home_kernel(code_ref, rows_ref, _, *outs):
    slots, tokens = rows_ref.shape[0], outs[0].shape[0]
    chosen = lax.broadcasted_iota(jnp.int32, (slots, tokens), 0) == code_ref[...]
    width = outs[0].shape[1]
    for i, out_ref in enumerate(outs):
        out_ref[...] = lax.dot_general(
            chosen.astype(BF16),
            rows_ref[:, i * width:(i + 1) * width],
            (((0,), (0,)), ((), ())),
            preferred_element_type=F32,
        ).astype(BF16)


def gradients_home(code, rows, token):
    half = jax.ShapeDtypeStruct((code.shape[0], rows.shape[1] // 2), BF16)
    return call(
        home_kernel, (half, half), [VMEM, VMEM, ANY], (VMEM, VMEM), [],
        4 << 27, 3 << 20, code.reshape(1, -1), rows, token,
    )


def load_any(slot, sem, info_ref, block, half, own, other, p1, f1, p2, f2, direct, crossed):
    y_lo, core, parity = info_ref[1], info_ref[2], info_ref[3]
    width = slot.shape[1]
    at = pl.ds(half * width, width)
    near, low = block // 2 == y_lo, block % 2
    for ref, same in ((own, low == core), (other, low != core)):
        @pl.when(jnp.logical_and(near, same))
        def _():
            pltpu.make_async_copy(ref.at[:, at], slot, sem).start()

    far = jnp.logical_not(near)
    for ref, same in ((direct, low == core), (crossed, low != core)):
        @pl.when(jnp.logical_and(far, same))
        def _():
            pltpu.make_async_copy(ref.at[:, at], slot.at[pl.ds(0, DIRECT)], sem).start()

    for ref, test in (
        (p1, jnp.logical_and(low == core, half == parity)),
        (f1, jnp.logical_and(low != core, half == parity)),
        (p2, jnp.logical_and(low == core, half != parity)),
        (f2, jnp.logical_and(low != core, half != parity)),
    ):
        @pl.when(jnp.logical_and(far, test))
        def _():
            pltpu.make_async_copy(ref, slot.at[pl.ds(DIRECT, ref.shape[0])], sem).start()


def back_kernel(steps, starts, ends, info_ref, *refs):
    refs = list(refs)
    grads = [refs.pop(0) for _ in steps]
    before = None if starts else refs.pop(0)
    slope_ref = refs.pop(0) if ends else None
    pieces = [refs.pop(0) for _ in range(8)]
    out_ref, buffer, sems = refs[-3:]
    z = info_ref[0]
    for i, (step, half) in enumerate(steps):
        load_any(buffer.at[i], sems.at[i], info_ref, (z + step) % 4, half, *pieces)
    total = None if starts else before[...]
    for i in range(len(steps)):
        pltpu.make_async_copy(buffer.at[i], buffer.at[i], sems.at[i]).wait()
        part = lax.dot_general(grads[i][...], buffer[i], (((1,), (1,)), ((), ())), preferred_element_type=F32)
        total = part if total is None else total + part
    out_ref[...] = (total * slope_ref[...]).astype(BF16) if ends else total


def back(info, steps, grads, before, slope, pieces, *tokens):
    rows, (depth, width) = grads[0].shape[0], pieces[0].shape
    extra = [a for a in (before, slope) if a is not None]
    out = jax.ShapeDtypeStruct((rows, depth), F32 if slope is None else BF16)
    return call(
        functools.partial(back_kernel, steps, before is None, slope is not None),
        out,
        [SMEM] + [VMEM] * (len(grads) + len(extra)) + [ANY] * (8 + len(tokens)), VMEM,
        [pltpu.VMEM((len(steps), depth, width // 2), BF16), pltpu.SemaphoreType.DMA((len(steps),))],
        len(steps) * 7 << 27, len(steps) * 3 << 20,
        info, *grads, *extra, *pieces, *tokens, limit=46,
    )


def body(patches, norm_gain, w_in, b_in, w_out, b_out, text_rows, dest_group, dest_row, grad_rows):
    seq = lax.axis_index("seq")
    core, y_lo = seq % 2, seq // 2
    parity = (lax.axis_index("section") // 2) % 2
    z = lax.axis_index("tensor")
    info = jnp.stack([z, y_lo, core, parity]).astype(jnp.int32)

    count = dest_row.shape[0]
    groups = lax.axis_size(PLANE)
    capacity = max(2, 2 * count // groups)
    width = grad_rows.shape[1]
    target = dest_group.reshape(-1)
    member = (target[:, None] == jnp.arange(groups, dtype=jnp.int32)[None, :]).astype(jnp.int32)
    slot_of = jnp.sum((jnp.cumsum(member, axis=0) - 1) * member, axis=1)
    code = target * capacity + slot_of
    chosen = jnp.arange(groups * capacity, dtype=jnp.int32)[:, None] == code[None, :]
    send_rows = jnp.sum(jnp.where(chosen, dest_row[None, :] + 1, 0), axis=1) - 1
    swap = functools.partial(lax.all_to_all, axis_name=PLANE, split_axis=0, concat_axis=0, tiled=True)
    named = swap(send_rows.reshape(groups, capacity))
    got_rows = named.reshape(1, groups * capacity)

    rows, cols = w_in.shape
    p1_in = move(parts_of(info, w_in, [(None, rows // 2, 0, cols)])[0], ALONG_Y)
    other_in = move(w_in, CORE)
    other_out = move(w_out, CORE)
    x = patches.T
    size = x.shape[0] // 2
    xa, xb = up(x), down(x)
    xc1, xc2 = up(xa[:size]), down(xb[size:])
    rows, cols = w_out.shape
    relayed, straight = parts_of(
        info, w_out, [(DIRECT, rows - DIRECT, None, cols // 2), (0, DIRECT, 0, cols)]
    )
    p1_in = after(p1_in, relayed, other_in, other_out, named, xa, xb)
    p2_in = move(p1_in, ALONG_X)
    f1_in = move(p1_in, CORE)
    p1 = move(after(relayed, p1_in), ALONG_Y)
    picked, picked_token = pick_rows(got_rows, grad_rows)
    merged, merged_token = merge(info, norm_gain, x, (xa, xb, xc1, xc2))
    total, first_token = first_near(info, merged, (w_in, other_in))
    p2_in = after(p2_in, first_token, picked_token)
    p2 = move(p1, ALONG_X)
    f1 = move(p1, CORE)
    direct = move(after(straight, p1), ALONG_Y)

    hidden, slope = first_far(info, merged, b_in, total, (p1_in, f1_in, p2_in, move(p2_in, CORE)))
    near, near_token = near_blocks(info, hidden, w_out, other_out)
    p2, direct = after(p2, near_token), after(direct, near_token)
    picked = after(picked, p2, direct)
    f2 = move(p2, CORE)
    crossed = move(direct, CORE)
    t20, t21, t10, t11, t30, t31, t00, t01 = far_terms(info, hidden, near, (p1, f1, p2, f2, direct, crossed))

    returned = swap(picked.reshape(groups, capacity, width)).reshape(groups * capacity, width)

    def add(one, two):
        return (one.astype(F32) + two.astype(F32)).astype(BF16)

    sa1, sa2 = up(t20), down(t21)
    sb1, sb2 = up(t11), down(t30)
    sc1, sc2 = up(add(t10, sa1)), down(add(t31, sa2))
    g1, g2 = gradients_home(code, returned, sb1)
    send = rows_to_send(code, b_out, g1, (t00, sb2, sc1, t01, sb1, sc2), groups * capacity)
    got = swap(send.reshape(groups, capacity, width)).reshape(groups * capacity, width)

    ga1, ga2 = up(g1), down(g2)
    gb1, gb2 = up(g2), down(g1)
    pieces = (w_out, other_out, p1, f1, p2, f2, direct, crossed)
    total = back(info, ((0, 0), (0, 1)), (g1, g2), None, None, pieces)
    gc1, gc2 = up(after(ga1, total)), down(after(ga2, total))
    total = back(info, ((3, 0), (1, 1)), (ga1, ga2), total, None, pieces)
    llm_input, placed = place_rows(got_rows, text_rows, got)
    grad_hidden = back(
        info, ((3, 1), (1, 0), (2, 0), (2, 1)), (gb1, gb2, gc1, gc2), total, slope, pieces, placed
    )
    return (llm_input, grad_hidden)


def solution(mesh):
    in_specs = (
        P(("section", "seq"), "tensor"),
        P(),
        P("seq", "tensor"),
        P("tensor"),
        P("tensor", "seq"),
        P("tensor"),
        P(("section", "seq"), "tensor"),
        P(("section", "seq"), None),
        P(("section", "seq")),
        P(("section", "seq"), "tensor"),
    )
    out_specs = (P(("section", "seq"), "tensor"), P(("section", "seq"), "tensor"))
    return jax.shard_map(body, mesh=mesh, in_specs=in_specs, out_specs=out_specs, check_vma=False)
```

```python
import functools

import jax
import jax.numpy as jnp
from jax import lax
from jax.experimental import pallas as pl
from jax.experimental.pallas import tpu as pltpu
from jax.sharding import PartitionSpec as P

PLANE = ("section", "seq")
VMEM = pl.BlockSpec(memory_space=pltpu.VMEM)
SMEM = pl.BlockSpec(memory_space=pltpu.SMEM)
ANY = pl.BlockSpec(memory_space=pl.ANY)
BF16, F32 = jnp.bfloat16, jnp.float32
DIRECT = 416


TOKEN = jax.ShapeDtypeStruct((8, 128), F32)


def spot(x, y, c):
    return ((x % 4) * 4 + (y % 4)) * 2 + c


CHIPS = [(x, y, c) for x in range(4) for y in range(4) for c in range(2)]
CORE = [(spot(x, y, c), spot(x, y, 1 - c)) for x, y, c in CHIPS]
ALONG_Y = [(spot(x, y, c), spot(x, y + 1 - 2 * c, c)) for x, y, c in CHIPS]
ALONG_X = [(spot(x, y, c), spot(x + 1 - 2 * c, y, c)) for x, y, c in CHIPS]


def move(value, pairs):
    return lax.ppermute(value, PLANE, pairs)


def up(value):
    return lax.ppermute(value, "tensor", [(z, (z + 1) % 4) for z in range(4)])


def down(value):
    return lax.ppermute(value, "tensor", [(z, (z + 3) % 4) for z in range(4)])


def after(value, *others):
    return pl.pallas_call(
        lambda *refs: None,
        out_shape=jax.ShapeDtypeStruct(value.shape, value.dtype),
        in_specs=[ANY] * (1 + len(others)),
        out_specs=ANY,
        input_output_aliases={0: 0},
    )(value, *others)


def call(kernel, out_shape, in_specs, out_specs, scratch, flops, moved, *args, limit=46):
    return pl.pallas_call(
        kernel,
        out_shape=out_shape,
        in_specs=in_specs,
        out_specs=out_specs,
        scratch_shapes=scratch,
        compiler_params=pltpu.CompilerParams(vmem_limit_bytes=limit << 20),
        cost_estimate=pl.CostEstimate(flops=flops, bytes_accessed=moved, transcendentals=0),
    )(*args)


def parts_kernel(cuts, info_ref, own_ref, *refs):
    outs, sems = refs[-1 - len(cuts):-1], refs[-1]
    copies = []
    for i, (low, rows, left, cols) in enumerate(cuts):
        if low is None:
            low = pl.multiple_of(info_ref[3] * rows, rows)
        if left is None:
            left = pl.multiple_of(info_ref[3] * cols, cols)
        from_ref = own_ref.at[pl.ds(low, rows), pl.ds(left, cols)]
        copies.append(pltpu.make_async_copy(from_ref, outs[i], sems.at[i]))
    for copy in copies:
        copy.start()
    for copy in copies:
        copy.wait()


def parts_of(info, own, cuts, *tokens):
    out = [jax.ShapeDtypeStruct((rows, cols), BF16) for _, rows, _, cols in cuts]
    return call(
        functools.partial(parts_kernel, cuts), out, [SMEM] + [ANY] * (1 + len(tokens)), [VMEM] * len(out),
        [pltpu.SemaphoreType.DMA((len(out),))], 0, 2 * own.size, info, own, *tokens,
    )


def merge_kernel(info_ref, gain_ref, own_ref, *refs):
    parts, (out_ref, token_ref, x_ref, sems) = refs[:4], refs[4:]
    token_ref[...] = jnp.zeros_like(token_ref)
    z = info_ref[0]
    size = own_ref.shape[0] // 2
    width = 8 * size
    copies = []
    for i, (ref, step, half) in enumerate(zip((own_ref, *parts), (0, 3, 1, 2, 2), (0, 0, 0, 0, 1))):
        at = pl.multiple_of(((z + step) % 4) * 2 * size + half * size, 32)
        copies.append(pltpu.make_async_copy(ref, x_ref.at[pl.ds(at, ref.shape[0])], sems.at[i]))
    for copy in copies:
        copy.start()
    for copy in copies:
        copy.wait()
    rows = 256
    tokens = rows // 4
    r = lax.broadcasted_iota(jnp.int32, (rows, rows), 1)
    q = lax.broadcasted_iota(jnp.int32, (rows, rows), 0)
    pick = (r == (q % tokens) * 4 + q // tokens).astype(BF16)
    for j in range(x_ref.shape[1] // rows):
        v = lax.dot_general(
            pick, x_ref[:, j * rows:(j + 1) * rows], (((1,), (1,)), ((), ())), preferred_element_type=F32
        )
        scale = lax.rsqrt(jnp.mean(v * v, axis=-1, keepdims=True) + 1e-06)
        n = (v * scale * gain_ref[...]).astype(BF16)
        for p in range(4):
            out_ref[j * tokens:(j + 1) * tokens, p * width:(p + 1) * width] = n[p * tokens:(p + 1) * tokens]


def merge(info, gain, own, parts):
    width, rows = 4 * own.shape[0], own.shape[1]
    return call(
        merge_kernel,
        (jax.ShapeDtypeStruct((rows // 4, 4 * width), BF16), TOKEN),
        [SMEM, VMEM] + [ANY] * 5, (VMEM, VMEM),
        [pltpu.VMEM((width, rows), BF16), pltpu.SemaphoreType.DMA((5,))],
        1 << 30, 6 << 20,
        info, gain.reshape(1, -1), own, *parts,
    )


def load_parts(jobs, buffer, sems):
    copies = [pltpu.make_async_copy(ref, buffer.at[i], sems.at[i]) for i, (ref, _, _) in enumerate(jobs)]
    for copy in copies:
        copy.start()
    return copies


def add_parts(jobs, copies, x_ref, buffer, total):
    depth = buffer.shape[1]
    for i, (copy, (_, block, half)) in enumerate(zip(copies, jobs)):
        copy.wait()
        at = pl.multiple_of((2 * block + half) * depth, 128)
        part = jnp.dot(x_ref[:, pl.ds(at, depth)], buffer[i], preferred_element_type=F32)
        total = part if total is None else total + part
    return total


def first_near_kernel(info_ref, x_ref, own_ref, other_ref, out_ref, token_ref, buffer, sems):
    token_ref[...] = jnp.zeros_like(token_ref)
    y_lo, core = info_ref[1], info_ref[2]
    depth = buffer.shape[1]
    jobs = [
        (ref.at[pl.ds(half * depth, depth)], 2 * y_lo + low, half)
        for ref, low in ((own_ref, core), (other_ref, 1 - core)) for half in range(2)
    ]
    out_ref[...] = add_parts(jobs, load_parts(jobs, buffer, sems), x_ref, buffer, None)


def first_far_kernel(info_ref, x_ref, b_ref, near_ref, p1, f1, p2, f2, hidden_ref, slope_ref, buffer, sems):
    y_lo, core, parity = info_ref[1], info_ref[2], info_ref[3]
    far = 2 - 2 * y_lo
    jobs = [
        (p1, far + core, parity), (f1, far + 1 - core, parity),
        (p2, far + core, 1 - parity), (f2, far + 1 - core, 1 - parity),
    ]
    pre = add_parts(jobs, load_parts(jobs, buffer, sems), x_ref, buffer, near_ref[...] + b_ref[...])
    phi = 0.5 * (1.0 + lax.erf(pre * 0.7071067811865476))
    hidden_ref[...] = (pre * phi).astype(BF16)
    slope_ref[...] = phi + pre * jnp.exp(-0.5 * pre * pre) * 0.3989422804014327


def first_scratch(depth, cols):
    return [pltpu.VMEM((4, depth, cols), BF16), pltpu.SemaphoreType.DMA((4,))]


def first_near(info, x, near):
    rows, (depth, cols) = x.shape[0], near[0].shape
    return call(
        first_near_kernel,
        (jax.ShapeDtypeStruct((rows, cols), F32), TOKEN),
        [SMEM, VMEM, ANY, ANY], (VMEM, VMEM), first_scratch(depth // 2, cols), 17 << 27, 9 << 20,
        info, x, *near,
    )


def first_far(info, x, b, total, far):
    rows, (depth, cols) = x.shape[0], far[0].shape
    return call(
        first_far_kernel,
        (jax.ShapeDtypeStruct((rows, cols), BF16), jax.ShapeDtypeStruct((rows, cols), F32)),
        [SMEM, VMEM, VMEM, VMEM] + [ANY] * 4, (VMEM, VMEM), first_scratch(depth, cols), 17 << 27, 12 << 20,
        info, x, b.reshape(1, -1), total, *far,
    )


def near_kernel(info_ref, h_ref, own_ref, other_ref, out_ref, token_ref, buffer, sems):
    token_ref[...] = jnp.zeros_like(token_ref)
    core = info_ref[2]
    width = buffer.shape[2]
    jobs = [(ref, low, half) for ref, low in ((own_ref, core), (other_ref, 1 - core)) for half in range(2)]
    copies = [
        pltpu.make_async_copy(ref.at[:, pl.ds(half * width, width)], buffer.at[i], sems.at[i])
        for i, (ref, _, half) in enumerate(jobs)
    ]
    for copy in copies:
        copy.start()
    for i, (copy, (_, low, half)) in enumerate(zip(copies, jobs)):
        copy.wait()
        part = jnp.dot(h_ref[...], buffer[i], preferred_element_type=F32)
        out_ref[low, :, half * width:(half + 1) * width] = part.astype(BF16)


def far_kernel(info_ref, h_ref, near_ref, p1, f1, p2, f2, direct, crossed, *refs):
    outs, (buffer, whole, held, sems, out_sems) = refs[:8], refs[8:]
    z, y_lo, core, parity = info_ref[0], info_ref[1], info_ref[2], info_ref[3]
    width = buffer.shape[2]
    jobs = [
        (p1, core, parity), (f1, 1 - core, parity), (p2, core, 1 - parity), (f2, 1 - core, 1 - parity),
    ]
    for i, (ref, low, half) in enumerate(jobs):
        at = pl.ds(pl.multiple_of(half * width, width), width)
        straight = (direct, crossed)[i % 2].at[:, at]
        pltpu.make_async_copy(ref, buffer.at[i, pl.ds(DIRECT, ref.shape[0])], sems.at[i]).start()
        pltpu.make_async_copy(straight, buffer.at[i, pl.ds(0, DIRECT)], sems.at[i]).start()
    here = pltpu.make_async_copy(near_ref, whole.at[pl.ds(2 * y_lo, 2)], sems.at[4])
    hidden = pltpu.make_async_copy(h_ref, held, sems.at[5])
    hidden.start()
    here.start()
    hidden.wait()
    for i, (_, low, half) in enumerate(jobs):
        pltpu.make_async_copy(buffer.at[i], buffer.at[i], sems.at[i]).wait()
        part = jnp.dot(held[...], buffer[i], preferred_element_type=F32)
        at = pl.multiple_of(half * width, width)
        whole[2 - 2 * y_lo + low, :, pl.ds(at, width)] = part.astype(BF16)
    here.wait()
    copies = []
    for i, step in enumerate((2, 1, 3, 0)):
        for half in range(2):
            from_ref = whole.at[(z + step) % 4, :, pl.ds(half * width, width)]
            copies.append(pltpu.make_async_copy(from_ref, outs[2 * i + half], out_sems.at[2 * i + half]))
    for copy in copies:
        copy.start()
    for copy in copies:
        copy.wait()


def far_terms(info, h, near, pieces):
    rows, width = near.shape[1:]
    out = jax.ShapeDtypeStruct((rows, width // 2), BF16)
    return call(
        far_kernel,
        [out] * 8,
        [SMEM, ANY, ANY] + [ANY] * 6, [ANY] * 8,
        [
            pltpu.VMEM((4, h.shape[1], width // 2), BF16),
            pltpu.VMEM((4, rows, width), BF16),
            pltpu.VMEM(h.shape, BF16),
            pltpu.SemaphoreType.DMA((6,)),
            pltpu.SemaphoreType.DMA((8,)),
        ],
        27 << 27, 17 << 20,
        info, h, near, *pieces,
    )


def near_blocks(info, h, own, other):
    rows, width = own.shape
    return call(
        near_kernel,
        (jax.ShapeDtypeStruct((2, h.shape[0], width), BF16), TOKEN),
        [SMEM, VMEM, ANY, ANY], (VMEM, VMEM),
        [pltpu.VMEM((4, rows, width // 2), BF16), pltpu.SemaphoreType.DMA((4,))],
        27 << 27, 13 << 20,
        info, h, own, other,
    )


def send_kernel(code_ref, bias_ref, _, *refs):
    parts, (out_ref, sum_ref) = refs[:6], refs[6:]
    half = parts[0].shape[1]
    for i in range(2):
        at = slice(i * half, (i + 1) * half)
        total = sum(ref[...].astype(F32) for ref in parts[3 * i:3 * i + 3])
        sum_ref[:, at] = (total + bias_ref[:, at]).astype(BF16)
    slots, tokens = out_ref.shape[0], sum_ref.shape[0]
    chosen = lax.broadcasted_iota(jnp.int32, (slots, tokens), 0) == code_ref[...]
    out_ref[...] = jnp.dot(chosen.astype(BF16), sum_ref[...], preferred_element_type=F32).astype(BF16)


def rows_to_send(code, bias, token, parts, slots):
    rows, half = parts[0].shape
    return call(
        send_kernel,
        jax.ShapeDtypeStruct((slots, 2 * half), BF16),
        [VMEM, VMEM, ANY] + [VMEM] * 6, VMEM, [pltpu.VMEM((rows, 2 * half), BF16)],
        4 << 27, 6 << 20,
        code.reshape(1, -1), bias.reshape(1, -1), token, *parts,
    )


def pick_kernel(at_ref, rows_ref, out_ref, token_ref):
    token_ref[...] = jnp.zeros_like(token_ref)
    slots, rows = out_ref.shape[0], rows_ref.shape[0]
    named = (lax.broadcasted_iota(jnp.int32, (rows, slots), 0) == at_ref[...]).astype(BF16)
    out_ref[...] = lax.dot_general(
        named, rows_ref[...], (((0,), (0,)), ((), ())), preferred_element_type=F32
    ).astype(BF16)


def pick_rows(at, rows):
    slots, (count, width) = at.shape[1], rows.shape
    step = width // 4
    return pl.pallas_call(
        pick_kernel,
        grid=(4,),
        out_shape=(jax.ShapeDtypeStruct((slots, width), BF16), TOKEN),
        in_specs=[pl.BlockSpec((1, slots), lambda i: (0, 0)), pl.BlockSpec((count, step), lambda i: (0, i))],
        out_specs=(pl.BlockSpec((slots, step), lambda i: (0, i)), pl.BlockSpec((8, 128), lambda i: (0, 0))),
        compiler_params=pltpu.CompilerParams(vmem_limit_bytes=61 << 20),
        cost_estimate=pl.CostEstimate(flops=16 << 27, bytes_accessed=6 << 20, transcendentals=0),
    )(at, rows)


def place_kernel(at_ref, text_ref, got_ref, out_ref, token_ref):
    token_ref[...] = jnp.zeros_like(token_ref)
    rows, slots = out_ref.shape[0], got_ref.shape[0]
    row = lax.broadcasted_iota(jnp.int32, (rows, slots), 0) + pl.program_id(0) * rows
    added = jnp.dot((row == at_ref[...]).astype(BF16), got_ref[...], preferred_element_type=F32)
    out_ref[...] = (text_ref[...].astype(F32) + added).astype(BF16)


def place_rows(at, text, got):
    (count, width), slots = text.shape, got.shape[0]
    step = count // 4
    return pl.pallas_call(
        place_kernel,
        grid=(4,),
        out_shape=(jax.ShapeDtypeStruct(text.shape, BF16), TOKEN),
        in_specs=[
            pl.BlockSpec((1, slots), lambda i: (0, 0)),
            pl.BlockSpec((step, width), lambda i: (i, 0)),
            pl.BlockSpec((slots, width), lambda i: (0, 0)),
        ],
        out_specs=(pl.BlockSpec((step, width), lambda i: (i, 0)), pl.BlockSpec((8, 128), lambda i: (0, 0))),
        compiler_params=pltpu.CompilerParams(vmem_limit_bytes=56 << 20),
        cost_estimate=pl.CostEstimate(flops=16 << 27, bytes_accessed=10 << 20, transcendentals=0),
    )(at, text, got)


def home_kernel(code_ref, rows_ref, _, *outs):
    slots, tokens = rows_ref.shape[0], outs[0].shape[0]
    chosen = lax.broadcasted_iota(jnp.int32, (slots, tokens), 0) == code_ref[...]
    width = outs[0].shape[1]
    for i, out_ref in enumerate(outs):
        out_ref[...] = lax.dot_general(
            chosen.astype(BF16),
            rows_ref[:, i * width:(i + 1) * width],
            (((0,), (0,)), ((), ())),
            preferred_element_type=F32,
        ).astype(BF16)


def gradients_home(code, rows, token):
    half = jax.ShapeDtypeStruct((code.shape[0], rows.shape[1] // 2), BF16)
    return call(
        home_kernel, (half, half), [VMEM, VMEM, ANY], (VMEM, VMEM), [],
        4 << 27, 3 << 20, code.reshape(1, -1), rows, token,
    )


def load_any(slot, sem, info_ref, block, half, own, other, p1, f1, p2, f2, direct, crossed):
    y_lo, core, parity = info_ref[1], info_ref[2], info_ref[3]
    width = slot.shape[1]
    at = pl.ds(half * width, width)
    near, low = block // 2 == y_lo, block % 2
    for ref, same in ((own, low == core), (other, low != core)):
        @pl.when(jnp.logical_and(near, same))
        def _():
            pltpu.make_async_copy(ref.at[:, at], slot, sem).start()

    far = jnp.logical_not(near)
    for ref, same in ((direct, low == core), (crossed, low != core)):
        @pl.when(jnp.logical_and(far, same))
        def _():
            pltpu.make_async_copy(ref.at[:, at], slot.at[pl.ds(0, DIRECT)], sem).start()

    for ref, test in (
        (p1, jnp.logical_and(low == core, half == parity)),
        (f1, jnp.logical_and(low != core, half == parity)),
        (p2, jnp.logical_and(low == core, half != parity)),
        (f2, jnp.logical_and(low != core, half != parity)),
    ):
        @pl.when(jnp.logical_and(far, test))
        def _():
            pltpu.make_async_copy(ref, slot.at[pl.ds(DIRECT, ref.shape[0])], sem).start()


def back_kernel(steps, starts, ends, info_ref, *refs):
    refs = list(refs)
    grads = [refs.pop(0) for _ in steps]
    before = None if starts else refs.pop(0)
    slope_ref = refs.pop(0) if ends else None
    pieces = [refs.pop(0) for _ in range(8)]
    out_ref, buffer, sems = refs[-3:]
    z = info_ref[0]
    for i, (step, half) in enumerate(steps):
        load_any(buffer.at[i], sems.at[i], info_ref, (z + step) % 4, half, *pieces)
    total = None if starts else before[...]
    for i in range(len(steps)):
        pltpu.make_async_copy(buffer.at[i], buffer.at[i], sems.at[i]).wait()
        part = lax.dot_general(grads[i][...], buffer[i], (((1,), (1,)), ((), ())), preferred_element_type=F32)
        total = part if total is None else total + part
    out_ref[...] = (total * slope_ref[...]).astype(BF16) if ends else total


def back(info, steps, grads, before, slope, pieces, *tokens):
    rows, (depth, width) = grads[0].shape[0], pieces[0].shape
    extra = [a for a in (before, slope) if a is not None]
    out = jax.ShapeDtypeStruct((rows, depth), F32 if slope is None else BF16)
    return call(
        functools.partial(back_kernel, steps, before is None, slope is not None),
        out,
        [SMEM] + [VMEM] * (len(grads) + len(extra)) + [ANY] * (8 + len(tokens)), VMEM,
        [pltpu.VMEM((len(steps), depth, width // 2), BF16), pltpu.SemaphoreType.DMA((len(steps),))],
        len(steps) * 7 << 27, len(steps) * 3 << 20,
        info, *grads, *extra, *pieces, *tokens, limit=46,
    )


def body(patches, norm_gain, w_in, b_in, w_out, b_out, text_rows, dest_group, dest_row, grad_rows):
    seq = lax.axis_index("seq")
    core, y_lo = seq % 2, seq // 2
    parity = (lax.axis_index("section") // 2) % 2
    z = lax.axis_index("tensor")
    info = jnp.stack([z, y_lo, core, parity]).astype(jnp.int32)

    count = dest_row.shape[0]
    groups = lax.axis_size(PLANE)
    capacity = max(2, 2 * count // groups)
    width = grad_rows.shape[1]
    target = dest_group.reshape(-1)
    member = (target[:, None] == jnp.arange(groups, dtype=jnp.int32)[None, :]).astype(jnp.int32)
    slot_of = jnp.sum((jnp.cumsum(member, axis=0) - 1) * member, axis=1)
    code = target * capacity + slot_of
    chosen = jnp.arange(groups * capacity, dtype=jnp.int32)[:, None] == code[None, :]
    send_rows = jnp.sum(jnp.where(chosen, dest_row[None, :] + 1, 0), axis=1) - 1
    swap = functools.partial(lax.all_to_all, axis_name=PLANE, split_axis=0, concat_axis=0, tiled=True)
    named = swap(send_rows.reshape(groups, capacity))
    got_rows = named.reshape(1, groups * capacity)

    rows, cols = w_in.shape
    p1_in = move(parts_of(info, w_in, [(None, rows // 2, 0, cols)])[0], ALONG_Y)
    other_in = move(w_in, CORE)
    other_out = move(w_out, CORE)
    x = patches.T
    size = x.shape[0] // 2
    xa, xb = up(x), down(x)
    xc1, xc2 = up(xa[:size]), down(xb[size:])
    rows, cols = w_out.shape
    relayed, straight = parts_of(
        info, w_out, [(DIRECT, rows - DIRECT, None, cols // 2), (0, DIRECT, 0, cols)]
    )
    p1_in = after(p1_in, relayed, other_in, other_out, named, xa, xb)
    p2_in = move(p1_in, ALONG_X)
    f1_in = move(p1_in, CORE)
    p1 = move(after(relayed, p1_in), ALONG_Y)
    picked, picked_token = pick_rows(got_rows, grad_rows)
    merged, merged_token = merge(info, norm_gain, x, (xa, xb, xc1, xc2))
    total, first_token = first_near(info, merged, (w_in, other_in))
    p2_in = after(p2_in, first_token, picked_token)
    p2 = move(p1, ALONG_X)
    f1 = move(p1, CORE)
    direct = move(after(straight, p1), ALONG_Y)

    hidden, slope = first_far(info, merged, b_in, total, (p1_in, f1_in, p2_in, move(p2_in, CORE)))
    near, near_token = near_blocks(info, hidden, w_out, other_out)
    p2, direct = after(p2, near_token), after(direct, near_token)
    picked = after(picked, p2, direct)
    f2 = move(p2, CORE)
    crossed = move(direct, CORE)
    t20, t21, t10, t11, t30, t31, t00, t01 = far_terms(info, hidden, near, (p1, f1, p2, f2, direct, crossed))

    returned = swap(picked.reshape(groups, capacity, width)).reshape(groups * capacity, width)

    def add(one, two):
        return (one.astype(F32) + two.astype(F32)).astype(BF16)

    sa1, sa2 = up(t20), down(t21)
    sb1, sb2 = up(t11), down(t30)
    sc1, sc2 = up(add(t10, sa1)), down(add(t31, sa2))
    g1, g2 = gradients_home(code, returned, sb1)
    send = rows_to_send(code, b_out, g1, (t00, sb2, sc1, t01, sb1, sc2), groups * capacity)
    got = swap(send.reshape(groups, capacity, width)).reshape(groups * capacity, width)

    ga1, ga2 = up(g1), down(g2)
    gb1, gb2 = up(g2), down(g1)
    pieces = (w_out, other_out, p1, f1, p2, f2, direct, crossed)
    total = back(info, ((0, 0), (0, 1)), (g1, g2), None, None, pieces)
    gc1, gc2 = up(after(ga1, total)), down(after(ga2, total))
    total = back(info, ((3, 0), (1, 1)), (ga1, ga2), total, None, pieces)
    llm_input, placed = place_rows(got_rows, text_rows, got)
    grad_hidden = back(
        info, ((3, 1), (1, 0), (2, 0), (2, 1)), (gb1, gb2, gc1, gc2), total, slope, pieces, placed
    )
    return (llm_input, grad_hidden)


def solution(mesh):
    in_specs = (
        P(("section", "seq"), "tensor"),
        P(),
        P("seq", "tensor"),
        P("tensor"),
        P("tensor", "seq"),
        P("tensor"),
        P(("section", "seq"), "tensor"),
        P(("section", "seq"), None),
        P(("section", "seq")),
        P(("section", "seq"), "tensor"),
    )
    out_specs = (P(("section", "seq"), "tensor"), P(("section", "seq"), "tensor"))
    return jax.shard_map(body, mesh=mesh, in_specs=in_specs, out_specs=out_specs, check_vma=False)
```

```python
import functools

import jax
import jax.numpy as jnp
from jax import lax
from jax.experimental import pallas as pl
from jax.experimental.pallas import tpu as pltpu
from jax.sharding import PartitionSpec as P

PLANE = ("section", "seq")
VMEM = pl.BlockSpec(memory_space=pltpu.VMEM)
SMEM = pl.BlockSpec(memory_space=pltpu.SMEM)
ANY = pl.BlockSpec(memory_space=pl.ANY)
BF16, F32 = jnp.bfloat16, jnp.float32
DIRECT = 416


TOKEN = jax.ShapeDtypeStruct((8, 128), F32)


def spot(x, y, c):
    return ((x % 4) * 4 + (y % 4)) * 2 + c


CHIPS = [(x, y, c) for x in range(4) for y in range(4) for c in range(2)]
CORE = [(spot(x, y, c), spot(x, y, 1 - c)) for x, y, c in CHIPS]
ALONG_Y = [(spot(x, y, c), spot(x, y + 1 - 2 * c, c)) for x, y, c in CHIPS]
ALONG_X = [(spot(x, y, c), spot(x + 1 - 2 * c, y, c)) for x, y, c in CHIPS]


def move(value, pairs):
    return lax.ppermute(value, PLANE, pairs)


def up(value):
    return lax.ppermute(value, "tensor", [(z, (z + 1) % 4) for z in range(4)])


def down(value):
    return lax.ppermute(value, "tensor", [(z, (z + 3) % 4) for z in range(4)])


def after(value, *others):
    return pl.pallas_call(
        lambda *refs: None,
        out_shape=jax.ShapeDtypeStruct(value.shape, value.dtype),
        in_specs=[ANY] * (1 + len(others)),
        out_specs=ANY,
        input_output_aliases={0: 0},
    )(value, *others)


def call(kernel, out_shape, in_specs, out_specs, scratch, flops, moved, *args, limit=46):
    return pl.pallas_call(
        kernel,
        out_shape=out_shape,
        in_specs=in_specs,
        out_specs=out_specs,
        scratch_shapes=scratch,
        compiler_params=pltpu.CompilerParams(vmem_limit_bytes=limit << 20),
        cost_estimate=pl.CostEstimate(flops=flops, bytes_accessed=moved, transcendentals=0),
    )(*args)


def parts_kernel(cuts, info_ref, own_ref, *refs):
    outs, sems = refs[-1 - len(cuts):-1], refs[-1]
    copies = []
    for i, (low, rows, left, cols) in enumerate(cuts):
        if low is None:
            low = pl.multiple_of(info_ref[3] * rows, rows)
        if left is None:
            left = pl.multiple_of(info_ref[3] * cols, cols)
        from_ref = own_ref.at[pl.ds(low, rows), pl.ds(left, cols)]
        copies.append(pltpu.make_async_copy(from_ref, outs[i], sems.at[i]))
    for copy in copies:
        copy.start()
    for copy in copies:
        copy.wait()


def parts_of(info, own, cuts, *tokens, limit=46):
    out = [jax.ShapeDtypeStruct((rows, cols), BF16) for _, rows, _, cols in cuts]
    return call(
        functools.partial(parts_kernel, cuts), out, [SMEM] + [ANY] * (1 + len(tokens)), [VMEM] * len(out),
        [pltpu.SemaphoreType.DMA((len(out),))], 0, 2 * own.size, info, own, *tokens, limit=limit,
    )


def merge_kernel(info_ref, gain_ref, own_ref, *refs):
    parts, (out_ref, token_ref, x_ref, sems) = refs[:4], refs[4:]
    token_ref[...] = jnp.zeros_like(token_ref)
    z = info_ref[0]
    size = own_ref.shape[0] // 2
    width = 8 * size
    copies = []
    for i, (ref, step, half) in enumerate(zip((own_ref, *parts), (0, 3, 1, 2, 2), (0, 0, 0, 0, 1))):
        at = pl.multiple_of(((z + step) % 4) * 2 * size + half * size, 32)
        copies.append(pltpu.make_async_copy(ref, x_ref.at[pl.ds(at, ref.shape[0])], sems.at[i]))
    for copy in copies:
        copy.start()
    for copy in copies:
        copy.wait()
    rows = 256
    tokens = rows // 4
    r = lax.broadcasted_iota(jnp.int32, (rows, rows), 1)
    q = lax.broadcasted_iota(jnp.int32, (rows, rows), 0)
    pick = (r == (q % tokens) * 4 + q // tokens).astype(BF16)
    for j in range(x_ref.shape[1] // rows):
        v = lax.dot_general(
            pick, x_ref[:, j * rows:(j + 1) * rows], (((1,), (1,)), ((), ())), preferred_element_type=F32
        )
        scale = lax.rsqrt(jnp.mean(v * v, axis=-1, keepdims=True) + 1e-06)
        n = (v * scale * gain_ref[...]).astype(BF16)
        for p in range(4):
            out_ref[j * tokens:(j + 1) * tokens, p * width:(p + 1) * width] = n[p * tokens:(p + 1) * tokens]


def merge(info, gain, own, parts):
    width, rows = 4 * own.shape[0], own.shape[1]
    return call(
        merge_kernel,
        (jax.ShapeDtypeStruct((rows // 4, 4 * width), BF16), TOKEN),
        [SMEM, VMEM] + [ANY] * 5, (VMEM, VMEM),
        [pltpu.VMEM((width, rows), BF16), pltpu.SemaphoreType.DMA((5,))],
        1 << 30, 6 << 20,
        info, gain.reshape(1, -1), own, *parts,
    )


def load_parts(jobs, buffer, sems):
    copies = [pltpu.make_async_copy(ref, buffer.at[i], sems.at[i]) for i, (ref, _, _) in enumerate(jobs)]
    for copy in copies:
        copy.start()
    return copies


def add_parts(jobs, copies, x_ref, buffer, total):
    depth = buffer.shape[1]
    for i, (copy, (_, block, half)) in enumerate(zip(copies, jobs)):
        copy.wait()
        at = pl.multiple_of((2 * block + half) * depth, 128)
        part = jnp.dot(x_ref[:, pl.ds(at, depth)], buffer[i], preferred_element_type=F32)
        total = part if total is None else total + part
    return total


def first_near_kernel(info_ref, x_ref, own_ref, other_ref, out_ref, token_ref, buffer, sems):
    token_ref[...] = jnp.zeros_like(token_ref)
    y_lo, core = info_ref[1], info_ref[2]
    depth = buffer.shape[1]
    jobs = [
        (ref.at[pl.ds(half * depth, depth)], 2 * y_lo + low, half)
        for ref, low in ((own_ref, core), (other_ref, 1 - core)) for half in range(2)
    ]
    out_ref[...] = add_parts(jobs, load_parts(jobs, buffer, sems), x_ref, buffer, None)


def first_far_kernel(info_ref, x_ref, b_ref, near_ref, p1, f1, p2, f2, hidden_ref, slope_ref, buffer, sems):
    y_lo, core, parity = info_ref[1], info_ref[2], info_ref[3]
    far = 2 - 2 * y_lo
    jobs = [
        (p1, far + core, parity), (f1, far + 1 - core, parity),
        (p2, far + core, 1 - parity), (f2, far + 1 - core, 1 - parity),
    ]
    pre = add_parts(jobs, load_parts(jobs, buffer, sems), x_ref, buffer, near_ref[...] + b_ref[...])
    phi = 0.5 * (1.0 + lax.erf(pre * 0.7071067811865476))
    hidden_ref[...] = (pre * phi).astype(BF16)
    slope_ref[...] = phi + pre * jnp.exp(-0.5 * pre * pre) * 0.3989422804014327


def first_scratch(depth, cols):
    return [pltpu.VMEM((4, depth, cols), BF16), pltpu.SemaphoreType.DMA((4,))]


def first_near(info, x, near):
    rows, (depth, cols) = x.shape[0], near[0].shape
    return call(
        first_near_kernel,
        (jax.ShapeDtypeStruct((rows, cols), F32), TOKEN),
        [SMEM, VMEM, ANY, ANY], (VMEM, VMEM), first_scratch(depth // 2, cols), 17 << 27, 9 << 20,
        info, x, *near,
    )


def first_far(info, x, b, total, far):
    rows, (depth, cols) = x.shape[0], far[0].shape
    return call(
        first_far_kernel,
        (jax.ShapeDtypeStruct((rows, cols), BF16), jax.ShapeDtypeStruct((rows, cols), F32)),
        [SMEM, VMEM, VMEM, VMEM] + [ANY] * 4, (VMEM, VMEM), first_scratch(depth, cols), 17 << 27, 12 << 20,
        info, x, b.reshape(1, -1), total, *far,
    )


def near_kernel(info_ref, h_ref, own_ref, other_ref, out_ref, token_ref, buffer, sems):
    token_ref[...] = jnp.zeros_like(token_ref)
    core = info_ref[2]
    width = buffer.shape[2]
    jobs = [(ref, low, half) for ref, low in ((own_ref, core), (other_ref, 1 - core)) for half in range(2)]
    copies = [
        pltpu.make_async_copy(ref.at[:, pl.ds(half * width, width)], buffer.at[i], sems.at[i])
        for i, (ref, _, half) in enumerate(jobs)
    ]
    for copy in copies:
        copy.start()
    for i, (copy, (_, low, half)) in enumerate(zip(copies, jobs)):
        copy.wait()
        part = jnp.dot(h_ref[...], buffer[i], preferred_element_type=F32)
        out_ref[low, :, half * width:(half + 1) * width] = part.astype(BF16)


def far_kernel(info_ref, h_ref, near_ref, p1, f1, p2, f2, direct, crossed, *refs):
    outs, (buffer, whole, held, sems, out_sems) = refs[:8], refs[8:]
    z, y_lo, core, parity = info_ref[0], info_ref[1], info_ref[2], info_ref[3]
    width = buffer.shape[2]
    jobs = [
        (p1, core, parity), (f1, 1 - core, parity), (p2, core, 1 - parity), (f2, 1 - core, 1 - parity),
    ]
    for i, (ref, low, half) in enumerate(jobs):
        at = pl.ds(pl.multiple_of(half * width, width), width)
        straight = (direct, crossed)[i % 2].at[:, at]
        pltpu.make_async_copy(ref, buffer.at[i, pl.ds(DIRECT, ref.shape[0])], sems.at[i]).start()
        pltpu.make_async_copy(straight, buffer.at[i, pl.ds(0, DIRECT)], sems.at[i]).start()
    here = pltpu.make_async_copy(near_ref, whole.at[pl.ds(2 * y_lo, 2)], sems.at[4])
    hidden = pltpu.make_async_copy(h_ref, held, sems.at[5])
    hidden.start()
    here.start()
    hidden.wait()
    for i, (_, low, half) in enumerate(jobs):
        pltpu.make_async_copy(buffer.at[i], buffer.at[i], sems.at[i]).wait()
        part = jnp.dot(held[...], buffer[i], preferred_element_type=F32)
        at = pl.multiple_of(half * width, width)
        whole[2 - 2 * y_lo + low, :, pl.ds(at, width)] = part.astype(BF16)
    here.wait()
    copies = []
    for i, step in enumerate((2, 1, 3, 0)):
        for half in range(2):
            from_ref = whole.at[(z + step) % 4, :, pl.ds(half * width, width)]
            copies.append(pltpu.make_async_copy(from_ref, outs[2 * i + half], out_sems.at[2 * i + half]))
    for copy in copies:
        copy.start()
    for copy in copies:
        copy.wait()


def far_terms(info, h, near, pieces):
    rows, width = near.shape[1:]
    out = jax.ShapeDtypeStruct((rows, width // 2), BF16)
    return call(
        far_kernel,
        [out] * 8,
        [SMEM, ANY, ANY] + [ANY] * 6, [ANY] * 8,
        [
            pltpu.VMEM((4, h.shape[1], width // 2), BF16),
            pltpu.VMEM((4, rows, width), BF16),
            pltpu.VMEM(h.shape, BF16),
            pltpu.SemaphoreType.DMA((6,)),
            pltpu.SemaphoreType.DMA((8,)),
        ],
        27 << 27, 17 << 20,
        info, h, near, *pieces,
    )


def near_blocks(info, h, own, other):
    rows, width = own.shape
    return call(
        near_kernel,
        (jax.ShapeDtypeStruct((2, h.shape[0], width), BF16), TOKEN),
        [SMEM, VMEM, ANY, ANY], (VMEM, VMEM),
        [pltpu.VMEM((4, rows, width // 2), BF16), pltpu.SemaphoreType.DMA((4,))],
        27 << 27, 13 << 20,
        info, h, own, other,
    )


def send_kernel(code_ref, bias_ref, _, *refs):
    parts, (out_ref, sum_ref) = refs[:6], refs[6:]
    half = parts[0].shape[1]
    for i in range(2):
        at = slice(i * half, (i + 1) * half)
        total = sum(ref[...].astype(F32) for ref in parts[3 * i:3 * i + 3])
        sum_ref[:, at] = (total + bias_ref[:, at]).astype(BF16)
    slots, tokens = out_ref.shape[0], sum_ref.shape[0]
    chosen = lax.broadcasted_iota(jnp.int32, (slots, tokens), 0) == code_ref[...]
    out_ref[...] = jnp.dot(chosen.astype(BF16), sum_ref[...], preferred_element_type=F32).astype(BF16)


def rows_to_send(code, bias, token, parts, slots):
    rows, half = parts[0].shape
    return call(
        send_kernel,
        jax.ShapeDtypeStruct((slots, 2 * half), BF16),
        [VMEM, VMEM, ANY] + [VMEM] * 6, VMEM, [pltpu.VMEM((rows, 2 * half), BF16)],
        4 << 27, 6 << 20,
        code.reshape(1, -1), bias.reshape(1, -1), token, *parts,
    )


def pick_kernel(at_ref, rows_ref, out_ref, token_ref):
    token_ref[...] = jnp.zeros_like(token_ref)
    slots, rows = out_ref.shape[0], rows_ref.shape[0]
    named = (lax.broadcasted_iota(jnp.int32, (rows, slots), 0) == at_ref[...]).astype(BF16)
    out_ref[...] = lax.dot_general(
        named, rows_ref[...], (((0,), (0,)), ((), ())), preferred_element_type=F32
    ).astype(BF16)


def pick_rows(at, rows):
    slots, (count, width) = at.shape[1], rows.shape
    step = width // 4
    return pl.pallas_call(
        pick_kernel,
        grid=(4,),
        out_shape=(jax.ShapeDtypeStruct((slots, width), BF16), TOKEN),
        in_specs=[pl.BlockSpec((1, slots), lambda i: (0, 0)), pl.BlockSpec((count, step), lambda i: (0, i))],
        out_specs=(pl.BlockSpec((slots, step), lambda i: (0, i)), pl.BlockSpec((8, 128), lambda i: (0, 0))),
        compiler_params=pltpu.CompilerParams(vmem_limit_bytes=61 << 20),
        cost_estimate=pl.CostEstimate(flops=16 << 27, bytes_accessed=6 << 20, transcendentals=0),
    )(at, rows)


def place_kernel(at_ref, text_ref, got_ref, out_ref, token_ref):
    token_ref[...] = jnp.zeros_like(token_ref)
    rows, slots = out_ref.shape[0], got_ref.shape[0]
    row = lax.broadcasted_iota(jnp.int32, (rows, slots), 0) + pl.program_id(0) * rows
    added = jnp.dot((row == at_ref[...]).astype(BF16), got_ref[...], preferred_element_type=F32)
    out_ref[...] = (text_ref[...].astype(F32) + added).astype(BF16)


def place_rows(at, text, got):
    (count, width), slots = text.shape, got.shape[0]
    step = count // 4
    return pl.pallas_call(
        place_kernel,
        grid=(4,),
        out_shape=(jax.ShapeDtypeStruct(text.shape, BF16), TOKEN),
        in_specs=[
            pl.BlockSpec((1, slots), lambda i: (0, 0)),
            pl.BlockSpec((step, width), lambda i: (i, 0)),
            pl.BlockSpec((slots, width), lambda i: (0, 0)),
        ],
        out_specs=(pl.BlockSpec((step, width), lambda i: (i, 0)), pl.BlockSpec((8, 128), lambda i: (0, 0))),
        compiler_params=pltpu.CompilerParams(vmem_limit_bytes=56 << 20),
        cost_estimate=pl.CostEstimate(flops=16 << 27, bytes_accessed=10 << 20, transcendentals=0),
    )(at, text, got)


def home_kernel(code_ref, rows_ref, _, *outs):
    slots, tokens = rows_ref.shape[0], outs[0].shape[0]
    chosen = lax.broadcasted_iota(jnp.int32, (slots, tokens), 0) == code_ref[...]
    width = outs[0].shape[1]
    for i, out_ref in enumerate(outs):
        out_ref[...] = lax.dot_general(
            chosen.astype(BF16),
            rows_ref[:, i * width:(i + 1) * width],
            (((0,), (0,)), ((), ())),
            preferred_element_type=F32,
        ).astype(BF16)


def gradients_home(code, rows, token):
    half = jax.ShapeDtypeStruct((code.shape[0], rows.shape[1] // 2), BF16)
    return call(
        home_kernel, (half, half), [VMEM, VMEM, ANY], (VMEM, VMEM), [],
        4 << 27, 3 << 20, code.reshape(1, -1), rows, token,
    )


def load_any(slot, sem, info_ref, block, half, own, other, p1, f1, p2, f2, direct, crossed):
    y_lo, core, parity = info_ref[1], info_ref[2], info_ref[3]
    width = slot.shape[1]
    at = pl.ds(half * width, width)
    near, low = block // 2 == y_lo, block % 2
    for ref, same in ((own, low == core), (other, low != core)):
        @pl.when(jnp.logical_and(near, same))
        def _():
            pltpu.make_async_copy(ref.at[:, at], slot, sem).start()

    far = jnp.logical_not(near)
    for ref, same in ((direct, low == core), (crossed, low != core)):
        @pl.when(jnp.logical_and(far, same))
        def _():
            pltpu.make_async_copy(ref.at[:, at], slot.at[pl.ds(0, DIRECT)], sem).start()

    for ref, test in (
        (p1, jnp.logical_and(low == core, half == parity)),
        (f1, jnp.logical_and(low != core, half == parity)),
        (p2, jnp.logical_and(low == core, half != parity)),
        (f2, jnp.logical_and(low != core, half != parity)),
    ):
        @pl.when(jnp.logical_and(far, test))
        def _():
            pltpu.make_async_copy(ref, slot.at[pl.ds(DIRECT, ref.shape[0])], sem).start()


def back_kernel(steps, starts, ends, info_ref, *refs):
    refs = list(refs)
    grads = [refs.pop(0) for _ in steps]
    before = None if starts else refs.pop(0)
    slope_ref = refs.pop(0) if ends else None
    pieces = [refs.pop(0) for _ in range(8)]
    out_ref, buffer, sems = refs[-3:]
    z = info_ref[0]
    for i, (step, half) in enumerate(steps):
        load_any(buffer.at[i], sems.at[i], info_ref, (z + step) % 4, half, *pieces)
    total = None if starts else before[...]
    for i in range(len(steps)):
        pltpu.make_async_copy(buffer.at[i], buffer.at[i], sems.at[i]).wait()
        part = lax.dot_general(grads[i][...], buffer[i], (((1,), (1,)), ((), ())), preferred_element_type=F32)
        total = part if total is None else total + part
    out_ref[...] = (total * slope_ref[...]).astype(BF16) if ends else total


def back(info, steps, grads, before, slope, pieces, *tokens):
    rows, (depth, width) = grads[0].shape[0], pieces[0].shape
    extra = [a for a in (before, slope) if a is not None]
    out = jax.ShapeDtypeStruct((rows, depth), F32 if slope is None else BF16)
    return call(
        functools.partial(back_kernel, steps, before is None, slope is not None),
        out,
        [SMEM] + [VMEM] * (len(grads) + len(extra)) + [ANY] * (8 + len(tokens)), VMEM,
        [pltpu.VMEM((len(steps), depth, width // 2), BF16), pltpu.SemaphoreType.DMA((len(steps),))],
        len(steps) * 7 << 27, len(steps) * 3 << 20,
        info, *grads, *extra, *pieces, *tokens, limit=46,
    )


def body(patches, norm_gain, w_in, b_in, w_out, b_out, text_rows, dest_group, dest_row, grad_rows):
    seq = lax.axis_index("seq")
    core, y_lo = seq % 2, seq // 2
    parity = (lax.axis_index("section") // 2) % 2
    z = lax.axis_index("tensor")
    info = jnp.stack([z, y_lo, core, parity]).astype(jnp.int32)

    count = dest_row.shape[0]
    groups = lax.axis_size(PLANE)
    capacity = max(2, 2 * count // groups)
    width = grad_rows.shape[1]
    target = dest_group.reshape(-1)
    member = (target[:, None] == jnp.arange(groups, dtype=jnp.int32)[None, :]).astype(jnp.int32)
    slot_of = jnp.sum((jnp.cumsum(member, axis=0) - 1) * member, axis=1)
    code = target * capacity + slot_of
    chosen = jnp.arange(groups * capacity, dtype=jnp.int32)[:, None] == code[None, :]
    send_rows = jnp.sum(jnp.where(chosen, dest_row[None, :] + 1, 0), axis=1) - 1
    swap = functools.partial(lax.all_to_all, axis_name=PLANE, split_axis=0, concat_axis=0, tiled=True)
    named = swap(send_rows.reshape(groups, capacity))
    got_rows = named.reshape(1, groups * capacity)

    rows, cols = w_in.shape
    p1_in = move(parts_of(info, w_in, [(None, rows // 2, 0, cols)], limit=61)[0], ALONG_Y)
    other_in = move(w_in, CORE)
    other_out = move(w_out, CORE)
    x = patches.T
    size = x.shape[0] // 2
    xa, xb = up(x), down(x)
    xc1, xc2 = up(xa[:size]), down(xb[size:])
    rows, cols = w_out.shape
    relayed, straight = parts_of(
        info, w_out, [(DIRECT, rows - DIRECT, None, cols // 2), (0, DIRECT, 0, cols)]
    )
    p1_in = after(p1_in, relayed, other_in, other_out, named, xa, xb)
    p2_in = move(p1_in, ALONG_X)
    f1_in = move(p1_in, CORE)
    p1 = move(after(relayed, p1_in), ALONG_Y)
    picked, picked_token = pick_rows(got_rows, grad_rows)
    merged, merged_token = merge(info, norm_gain, x, (xa, xb, xc1, xc2))
    total, first_token = first_near(info, merged, (w_in, other_in))
    p2_in = after(p2_in, first_token, picked_token)
    p2 = move(p1, ALONG_X)
    f1 = move(p1, CORE)
    direct = move(after(straight, p1), ALONG_Y)

    hidden, slope = first_far(info, merged, b_in, total, (p1_in, f1_in, p2_in, move(p2_in, CORE)))
    near, near_token = near_blocks(info, hidden, w_out, other_out)
    p2, direct = after(p2, near_token), after(direct, near_token)
    picked = after(picked, p2, direct)
    f2 = move(p2, CORE)
    crossed = move(direct, CORE)
    t20, t21, t10, t11, t30, t31, t00, t01 = far_terms(info, hidden, near, (p1, f1, p2, f2, direct, crossed))

    returned = swap(picked.reshape(groups, capacity, width)).reshape(groups * capacity, width)

    def add(one, two):
        return (one.astype(F32) + two.astype(F32)).astype(BF16)

    sa1, sa2 = up(t20), down(t21)
    sb1, sb2 = up(t11), down(t30)
    sc1, sc2 = up(add(t10, sa1)), down(add(t31, sa2))
    g1, g2 = gradients_home(code, returned, sb1)
    send = rows_to_send(code, b_out, g1, (t00, sb2, sc1, t01, sb1, sc2), groups * capacity)
    got = swap(send.reshape(groups, capacity, width)).reshape(groups * capacity, width)

    ga1, ga2 = up(g1), down(g2)
    gb1, gb2 = up(g2), down(g1)
    pieces = (w_out, other_out, p1, f1, p2, f2, direct, crossed)
    total = back(info, ((0, 0), (0, 1)), (g1, g2), None, None, pieces)
    gc1, gc2 = up(after(ga1, total)), down(after(ga2, total))
    total = back(info, ((3, 0), (1, 1)), (ga1, ga2), total, None, pieces)
    llm_input, placed = place_rows(got_rows, text_rows, got)
    grad_hidden = back(
        info, ((3, 1), (1, 0), (2, 0), (2, 1)), (gb1, gb2, gc1, gc2), total, slope, pieces, placed
    )
    return (llm_input, grad_hidden)


def solution(mesh):
    in_specs = (
        P(("section", "seq"), "tensor"),
        P(),
        P("seq", "tensor"),
        P("tensor"),
        P("tensor", "seq"),
        P("tensor"),
        P(("section", "seq"), "tensor"),
        P(("section", "seq"), None),
        P(("section", "seq")),
        P(("section", "seq"), "tensor"),
    )
    out_specs = (P(("section", "seq"), "tensor"), P(("section", "seq"), "tensor"))
    return jax.shard_map(body, mesh=mesh, in_specs=in_specs, out_specs=out_specs, check_vma=False)
```
